128 devices in a mesh: row: 16 (over y, x_hi, core), col: 8 (over x_lo, z).
Axes of the slice: x: 4 (x_hi: 2, x_lo: 2; x = x_hi * 2 + x_lo), y: 4, z: 4, core: 2. Of those that a mesh axis runs over, the one named last changes fastest.
Arguments:
- tokens: bfloat16 [32, 16384], P(None, ('row', 'col')), may hold values from -40 to 40
- norm_gain: bfloat16 [16384], P('row'), may hold values from 0.099609375 to 1.8984375
- query_weight: bfloat16 [16384, 16384], P('row', 'col'), may hold values from -0.046875 to 0.046875
- keyval_weight: bfloat16 [16384, 2048], P('row', 'col'), may hold values from -0.046875 to 0.046875
- out_weight: bfloat16 [16384, 16384], P('col', 'row'), may hold values from -0.375 to 0.375
- key_cache: bfloat16 [32, 8192, 1024], P('row', None, 'col'), may hold values from -68 to 68
- value_cache: bfloat16 [32, 8192, 1024], P('row', None, 'col'), may hold values from -6 to 6
- lengths: int32 [32], P('row'), may hold values from 1 to 8192, as said below
- next_query: bfloat16 [16384, 16384], P(None, ('col', 'row')), may hold values from -0.046875 to 0.046875
Outputs:
- mixed: bfloat16 [32, 16384], P(None, ('row', 'col'))
- relaid: bfloat16 [16384, 16384], P('row', 'col')
The draws below stay inside these ranges and needn't reach their ends.
Inputs may be any that keep to these rules, and one draw needn't show every extreme that they name: `lengths`: one row holds exactly 8192 positions.
All inputs are finite; a program needn't handle non-finite values.
Results may differ from the reference program's by a relative error of at most 0.012.
The reference program's roundings to bfloat16 on the way count: a program that leaves them out, or rounds other values in their place, can miss the bound.
Values may be sent and summed in bfloat16 or wider, within the bound.
No kernel may reach another device: no remote copies, remote signals or barrier semaphores. Data moves between devices by JAX's collectives and lax.ppermute only.
A program may use at most 128 MiB of HBM per device.

```python
import math
import jax
import jax.numpy as jnp
from jax import lax

D = 16384
QH = 128
KVH = 8
HD = 128
CTX = 8192
TOKENS = 32


def draw_tokens(key, part):
    key = jax.random.fold_in(key, 11)
    first, second, third = jax.random.split(key, 3)
    position = jnp.arange(D).astype(jnp.float32) / D - 0.5
    entries = jnp.clip(jax.random.normal(first, (TOKENS, D), jnp.float32), -4.0, 4.0)
    feature_trend = 3.0 ** position
    row_scale = jnp.exp(jax.random.uniform(second, (TOKENS, 1), jnp.float32, math.log(0.3), math.log(3.0)))
    jitter = jnp.exp(jax.random.uniform(third, (1, D), jnp.float32, -0.6, 0.6))
    return (entries * row_scale * feature_trend[None, :] * jitter).astype(jnp.bfloat16)


def draw_key_cache(key, part):
    key = jax.random.fold_in(key, 23)
    first = jax.random.fold_in(key, 0)
    entries = jnp.clip(jax.random.normal(first, (TOKENS, CTX, KVH * HD), jnp.float32), -6.0, 6.0)
    return entries.astype(jnp.bfloat16)


def draw_lengths(key, part):
    key = jax.random.fold_in(key, 37)
    first, second = jax.random.split(key, 2)
    drawn = jax.random.randint(first, (TOKENS,), 1, CTX + 1)
    longest_row = jax.random.randint(second, (), 0, TOKENS)
    return jnp.where(jnp.arange(TOKENS) == longest_row, CTX, drawn).astype(jnp.int32)


def block_levels(rng, dims, shards, least, largest):
    factor_of, own = 1.0, jax.random.fold_in(rng, 6)
    for dim, blocks in shards:
        draws = jnp.exp(jax.random.uniform(jax.random.fold_in(own, dim), (blocks,), jnp.float32, least / len(shards), largest / len(shards)))
        factor_of = factor_of * jnp.repeat(draws, dims[dim] // blocks).reshape([-1 if axis == dim else 1 for axis in range(len(dims))])
    return factor_of


def centred(rng, dims, scale, bound, cuts=(), dtype=jnp.bfloat16):
    gain = block_levels(rng, dims, cuts, -0.22, 0.18) if cuts else 1.0
    values = jax.random.normal(rng, dims, jnp.float32) * scale * gain
    return jnp.minimum(jnp.maximum(values, -bound), bound).astype(dtype)


def setup_inputs(seed: int = 0) -> dict:
    key_of = jax.random.split(jax.random.key(seed), 10)
    tokens = draw_tokens(jax.random.fold_in(key_of[9], 71), 0)
    norm_gain = jnp.clip(1.0 + 0.18 * jax.random.normal(key_of[1], (D,), jnp.float32), 0.099609375, 1.8984375).astype(jnp.bfloat16)
    query_weight = centred(key_of[2], (D, QH * HD), D ** -0.5, 0.046875, ((0, 16), (1, 8)))
    keyval_weight = centred(key_of[3], (D, 2 * KVH * HD), D ** -0.5, 0.046875, ((0, 16), (1, 8)))
    out_weight = centred(key_of[4], (QH * HD, D), (2 * HD) ** -0.5, 0.375, ((0, 8), (1, 16)))
    key_cache = draw_key_cache(jax.random.fold_in(key_of[9], 71), 0)
    value_cache = centred(key_of[6], (TOKENS, CTX, KVH * HD), 1.0, 6.0, ((0, 16), (2, 8)))
    lengths = draw_lengths(jax.random.fold_in(key_of[9], 71), 0)
    next_query = centred(key_of[8], (D, QH * HD), D ** -0.5, 0.046875, ((1, 128),))
    return dict(tokens=tokens, norm_gain=norm_gain, query_weight=query_weight, keyval_weight=keyval_weight, out_weight=out_weight, key_cache=key_cache, value_cache=value_cache, lengths=lengths, next_query=next_query)


masked_score = -1e+30

def rotary(vectors, positions):
    half_dim = vectors.shape[-1] // 2
    freqs = 500000.0 ** (-(jnp.arange(half_dim).astype(jnp.float32) * 2.0 / vectors.shape[-1]))
    angles = positions.astype(jnp.float32)[:, None] * freqs[None, :]
    cosine = jnp.cos(angles)[:, None, :]
    sine_part = jnp.sin(angles)[:, None, :]
    front_half = vectors[..., :half_dim]
    back_half = vectors[..., half_dim:]
    return jnp.concatenate([front_half * cosine - back_half * sine_part, back_half * cosine + front_half * sine_part], axis=-1)

def attend_row(inputs):
    queries, new_key, new_value, key_rows, value_rows, length = inputs
    score_scale = HD ** (-0.5)
    query_f = queries.astype(jnp.float32)
    keys_f = key_rows.reshape(CTX, KVH, HD).astype(jnp.float32)
    values_f = value_rows.reshape(CTX, KVH, HD).astype(jnp.float32)
    scores = jnp.einsum('kgd,pkd->kgp', query_f, keys_f) * score_scale
    visible = jnp.arange(CTX) < length
    scores = jnp.where(visible[None, None, :], scores, masked_score)
    self_score = jnp.einsum('kgd,kd->kg', query_f, new_key.astype(jnp.float32)) * score_scale
    highest = jnp.maximum(lax.optimization_barrier(jnp.max(scores, axis=-1)), self_score)
    expos = jnp.exp(scores - highest[..., None])
    self_expo = jnp.exp(self_score - highest)
    totals = lax.optimization_barrier(jnp.sum(expos, axis=-1)) + self_expo
    rounded = lax.optimization_barrier(expos.astype(jnp.bfloat16)).astype(jnp.float32)
    numer = jnp.einsum('kgp,pkd->kgd', rounded, values_f) + self_expo[..., None] * new_value.astype(jnp.float32)[:, None, :]
    return (numer / totals[..., None]).astype(jnp.bfloat16).reshape(QH * HD)

def reference(tokens, norm_gain, query_weight, keyval_weight, out_weight, key_cache, value_cache, lengths, next_query):
    tokens_f = tokens.astype(jnp.float32)
    mean_square = lax.optimization_barrier(jnp.mean(tokens_f * tokens_f, axis=1))
    inv_scale = lax.rsqrt(mean_square + 1e-05)[:, None]
    normed = (tokens_f * norm_gain.astype(jnp.float32)[None, :]).astype(jnp.bfloat16)
    proj_query = jnp.dot(normed, query_weight, preferred_element_type=jnp.float32) * inv_scale
    proj_keyval = jnp.dot(normed, keyval_weight, preferred_element_type=jnp.float32) * inv_scale
    queries = rotary(proj_query.reshape(TOKENS, QH, HD), lengths).astype(jnp.bfloat16)
    queries = queries.reshape(TOKENS, KVH, QH // KVH, HD)
    keyval = proj_keyval.reshape(TOKENS, KVH, 2, HD)
    new_key = rotary(keyval[:, :, 0], lengths).astype(jnp.bfloat16)
    new_value = keyval[:, :, 1].astype(jnp.bfloat16)
    attended = lax.map(attend_row, (queries, new_key, new_value, key_cache, value_cache, lengths))
    mixed = jnp.dot(attended, out_weight, preferred_element_type=jnp.float32).astype(jnp.bfloat16)
    return (mixed, next_query)
```

```python
import functools

import jax
import jax.numpy as jnp
from jax import lax
from jax.experimental import pallas as pl
from jax.experimental.pallas import tpu as pltpu
from jax.sharding import PartitionSpec as P

HD = 128
masked_score = -1e30
SQUARES = 128
CHUNK = 1024

CORE, X_HALF, Y_NEAR, Y_FAR = 1, 2, 4, 12
Z_NEAR, Z_FAR, X_LOW = 1, 3, 4

COST = 1_000_000_000
VMEM = pl.BlockSpec(memory_space=pltpu.VMEM)
SMEM = pl.BlockSpec(memory_space=pltpu.SMEM)
HBM = pl.BlockSpec(memory_space=pltpu.HBM)
ANYWHERE = pl.BlockSpec(memory_space=pl.ANY)


def call(kernel, out, in_specs, out_specs, scratch=(), megabytes=16, cost=0.0, **options):
    return pl.pallas_call(
        kernel,
        out_shape=out,
        in_specs=in_specs,
        out_specs=out_specs,
        scratch_shapes=list(scratch),
        compiler_params=pltpu.CompilerParams(vmem_limit_bytes=megabytes << 20),
        cost_estimate=pl.CostEstimate(
            flops=int(cost * COST) + 1, bytes_accessed=1, transcendentals=0
        ),
        **options,
    )


def like(array, rows):
    return jax.ShapeDtypeStruct((rows,) + array.shape[1:], array.dtype)


def rotary_factors(positions, width):
    half_dim = width // 2
    freqs = 500000.0 ** (-(jnp.arange(half_dim).astype(jnp.float32) * 2.0 / width))
    angles = positions.astype(jnp.float32)[:, None] * freqs[None, :]
    cosine, sine = jnp.cos(angles), jnp.sin(angles)
    return (
        jnp.concatenate([cosine, cosine], axis=-1),
        jnp.concatenate([-sine, sine], axis=-1),
    )


def flip(block, axis, bits):
    size = lax.axis_size(axis)
    return lax.ppermute(block, axis, [(i, i ^ bits) for i in range(size)])


def shift_y(block, steps):
    size = lax.axis_size("row")
    return lax.ppermute(block, "row", [(i, (i + 4 * steps) % size) for i in range(size)])


def tie(*values):
    return lax.optimization_barrier(values)


def join_kernel(own_ref, other_ref, out_ref):
    rows = own_ref.shape[0]
    out_ref[:rows] = own_ref[...]
    out_ref[rows:] = other_ref[...]


def join(own, other, cost=0.0):
    both = like(own, 2 * own.shape[0])
    return call(join_kernel, both, [VMEM] * 2, VMEM, megabytes=2, cost=cost)(own, other)


def add_halves_kernel(kept_ref, got_ref, next_kept_ref, next_sent_ref):
    half = next_kept_ref.shape[0]
    next_kept_ref[...] = kept_ref[:half] + got_ref[:half]
    next_sent_ref[...] = kept_ref[half:] + got_ref[half:]


def add_halves(kept, got, cost=0.0):
    half = like(kept, kept.shape[0] // 2)
    return call(
        add_halves_kernel, [half, half], [VMEM] * 2, [VMEM] * 2, megabytes=2, cost=cost
    )(kept, got)


def gray(number):
    return number ^ (number >> 1)


def batch_row(me_ref, place):
    row = me_ref[0]
    y, x_half, core = row >> 2, (row >> 1) & 1, row & 1
    device = (
        ((y ^ gray((place >> 1) & 3)) << 2)
        | ((x_half ^ ((place >> 3) & 1)) << 1)
        | (core ^ (place >> 4))
    )
    return (device << 1) | (place & 1)


def project_kernel(
    me_ref, near_ref, far_ref, gain_ref, query_ref, keyval_ref, kept_ref, sent_ref, feats_scr
):
    half, rows = near_ref.shape[0], near_ref.shape[1]
    feats_scr[:half] = near_ref[...]
    feats_scr[half:] = far_ref[...]
    x_low, z = me_ref[1] >> 2, me_ref[1] & 3
    blocks = [
        feats_scr[gray((part & 3) ^ z) * 2 + ((part >> 2) ^ x_low)] for part in range(2 * half)
    ]
    shape = (rows, rows)
    order = batch_row(me_ref, lax.broadcasted_iota(jnp.int32, shape, 0))
    order = jnp.where(order == lax.broadcasted_iota(jnp.int32, shape, 1), 1.0, 0.0)
    feats = jnp.dot(
        order.astype(jnp.bfloat16),
        jnp.concatenate(blocks, axis=1),
        preferred_element_type=jnp.float32,
    )
    square_sum = jnp.sum(feats * feats, axis=1, keepdims=True)
    normed = (feats * gain_ref[...].astype(jnp.float32)).astype(jnp.bfloat16)
    columns = query_ref.shape[1]
    cut = rows // 2

    def put(start, values):
        end = start + values.shape[1]
        kept_ref[:, start:end] = values[:cut]
        sent_ref[:, start:end] = values[cut:]

    step = 512
    for start in range(0, columns, step):
        put(
            start,
            jnp.dot(
                normed, query_ref[:, start : start + step], preferred_element_type=jnp.float32
            ),
        )
    put(columns, jnp.dot(normed, keyval_ref[...], preferred_element_type=jnp.float32))
    put(columns + keyval_ref.shape[1], jnp.broadcast_to(square_sum, (rows, SQUARES)))


def project(me, near, far, gain, query_weight, keyval_weight):
    rows = near.shape[1]
    columns = query_weight.shape[1] + keyval_weight.shape[1] + SQUARES
    half = jax.ShapeDtypeStruct((rows // 2, columns), jnp.float32)
    return call(
        project_kernel,
        [half, half],
        [SMEM] + [VMEM] * 5,
        [VMEM] * 2,
        [pltpu.VMEM((2 * near.shape[0],) + near.shape[1:], near.dtype)],
        cost=2.5,
    )(me, near, far, gain[None], query_weight, keyval_weight)


def attend_kernel(
    features, lengths_ref, kept_ref, got_ref, cos_ref, sin_ref, key_ref, value_ref, out_ref,
    proj_scr, query_scr, score_scr, rows_scr,
):
    rows, positions, head_dim = key_ref.shape
    heads = query_scr.shape[0]
    query_cols = heads * head_dim
    scale = head_dim ** (-0.5)
    proj_scr[...] = kept_ref[...] + got_ref[...]

    def rotate(vectors, b):
        return vectors * cos_ref[b : b + 1] + pltpu.roll(vectors, head_dim // 2, 1) * sin_ref[
            b : b + 1
        ]

    for b in range(rows):
        squares = proj_scr[b : b + 1, -SQUARES:]
        inv_scale = lax.rsqrt(squares / features + 1e-05)
        for h in range(heads):
            query_scr[h : h + 1, :] = (
                proj_scr[b : b + 1, h * head_dim : (h + 1) * head_dim] * inv_scale
            )
        query = rotate(query_scr[...], b).astype(jnp.bfloat16)
        new_key = proj_scr[b : b + 1, query_cols : query_cols + head_dim] * inv_scale
        new_key = rotate(jnp.broadcast_to(new_key, (8, head_dim)), b)[:1].astype(jnp.bfloat16)
        new_value = proj_scr[b : b + 1, query_cols + head_dim : query_cols + 2 * head_dim]
        new_value = (new_value * inv_scale).astype(jnp.bfloat16).astype(jnp.float32)
        self_score = (
            jnp.sum(
                query.astype(jnp.float32) * new_key.astype(jnp.float32), axis=1, keepdims=True
            )
            * scale
        )
        length = lengths_ref[b]
        top = self_score
        for start in range(0, positions, CHUNK):
            scores = (
                lax.dot_general(
                    query,
                    key_ref[b, start : start + CHUNK, :],
                    (((1,), (1,)), ((), ())),
                    preferred_element_type=jnp.float32,
                )
                * scale
            )
            place = start + lax.broadcasted_iota(jnp.int32, scores.shape, 1)
            scores = jnp.where(place < length, scores, masked_score)
            score_scr[:, start : start + CHUNK] = scores
            top = jnp.maximum(top, jnp.max(scores, axis=1, keepdims=True))
        self_expo = jnp.exp(self_score - top)
        totals = self_expo
        numer = self_expo * new_value
        for start in range(0, positions, CHUNK):
            expos = jnp.exp(score_scr[:, start : start + CHUNK] - top)
            totals = totals + jnp.sum(expos, axis=1, keepdims=True)
            numer = numer + jnp.dot(
                expos.astype(jnp.bfloat16),
                value_ref[b, start : start + CHUNK, :],
                preferred_element_type=jnp.float32,
            )
        attended = numer / totals
        for h in range(heads):
            rows_scr[b : b + 1, h * head_dim : (h + 1) * head_dim] = attended[h : h + 1, :]
    out_ref[...] = rows_scr[...].astype(jnp.bfloat16)


def attend(lengths, kept, got, cosine, sine, key_cache, value_cache, features, heads):
    rows, positions, head_dim = key_cache.shape
    return call(
        functools.partial(attend_kernel, features),
        jax.ShapeDtypeStruct((rows, heads * head_dim), jnp.bfloat16),
        [SMEM] + [VMEM] * 6,
        VMEM,
        [
            pltpu.VMEM(kept.shape, jnp.float32),
            pltpu.VMEM((heads, head_dim), jnp.float32),
            pltpu.VMEM((heads, positions), jnp.float32),
            pltpu.VMEM((rows, heads * head_dim), jnp.float32),
        ],
    )(lengths, kept, got, cosine, sine, key_cache, value_cache)


def mix_kernel(me_ref, own_ref, other_ref, weight_ref, kept_ref, sent_ref, blocks_scr):
    rows = 2 * own_ref.shape[0]
    shape = (rows, rows)
    order = batch_row(me_ref, lax.broadcasted_iota(jnp.int32, shape, 1))
    order = jnp.where(order == lax.broadcasted_iota(jnp.int32, shape, 0), 1.0, 0.0)
    attended = jnp.dot(
        order.astype(jnp.bfloat16),
        jnp.concatenate([own_ref[...], other_ref[...]], axis=0),
        preferred_element_type=jnp.float32,
    ).astype(jnp.bfloat16)
    x_low, z = me_ref[1] >> 2, me_ref[1] & 3
    step, width = 256, kept_ref.shape[2]
    for start in range(0, weight_ref.shape[1], step):
        mixed = jnp.dot(
            attended, weight_ref[:, start : start + step], preferred_element_type=jnp.float32
        )
        for k in range(step // width):
            part = start // width + k
            place = gray((part & 3) ^ z) * 2 + ((part >> 2) ^ x_low)
            blocks_scr[place] = mixed[:, k * width : (k + 1) * width]
    half = kept_ref.shape[0]
    kept_ref[...] = blocks_scr[:half]
    sent_ref[...] = blocks_scr[half:]


def mix(me, own, other, out_weight):
    rows, width = 2 * own.shape[0], out_weight.shape[1] // 8
    half = jax.ShapeDtypeStruct((4, rows, width), jnp.float32)
    return call(
        mix_kernel,
        [half, half],
        [SMEM] + [VMEM] * 3,
        [VMEM] * 2,
        [pltpu.VMEM((8, rows, width), jnp.float32)],
    )(me, own, other, out_weight)


def start_and_wait(copies):
    for copy in copies:
        copy.start()
    for copy in copies:
        copy.wait()


def stage_kernel(groups, me_ref, chunks_ref, *refs):
    pieces, (buffer, in_sems, out_sems) = refs[: len(groups)], refs[len(groups) :]
    row = me_ref[0]
    copies = []
    for piece, group in zip(pieces, groups):
        for i, (dy, dx, other) in enumerate(group):
            chip = ((((row >> 2) + dy) & 3) << 1) | (((row >> 1) & 1) ^ dx)
            chunk = chunks_ref.at[(chip << 1) | ((row & 1) ^ other)]
            k = len(copies)
            copies.append(
                (
                    pltpu.make_async_copy(chunk, buffer.at[k], in_sems.at[k]),
                    pltpu.make_async_copy(buffer.at[k], piece.at[i], out_sems.at[k]),
                )
            )
    for fetch, _ in copies:
        fetch.start()
    for fetch, store in copies:
        fetch.wait()
        store.start()
    for _, store in copies:
        store.wait()


def stage(me, chunks, groups):
    count = sum(len(group) for group in groups)
    return call(
        functools.partial(stage_kernel, groups),
        [like(chunks, len(group)) for group in groups],
        [SMEM, HBM],
        [HBM] * len(groups),
        [
            pltpu.VMEM((count,) + chunks.shape[1:], chunks.dtype),
            pltpu.SemaphoreType.DMA((count,)),
            pltpu.SemaphoreType.DMA((count,)),
        ],
        60,
    )(me, chunks)


def pack_kernel(count, slots, *refs):
    pieces, out_ref, sems = refs[:count], refs[-2], refs[-1]
    start_and_wait(
        [
            pltpu.make_async_copy(pieces[p].at[i], out_ref.at[k], sems.at[k])
            for k, (p, i) in enumerate(slots)
        ]
    )


def pack(pieces, slots):
    return call(
        functools.partial(pack_kernel, len(pieces), slots),
        like(pieces[0], len(slots)),
        [ANYWHERE] * len(pieces),
        ANYWHERE,
        [pltpu.SemaphoreType.DMA((len(slots),))],
        1,
    )(*pieces)


def place_kernel(count, slots, me_ref, *refs):
    pieces, relaid_ref, sems = refs[:count], refs[-2], refs[-1]
    row = me_ref[0]
    copies = []
    for k, (piece, slot, dy, dx, other) in enumerate(slots):
        chip = ((((row >> 2) - dy) & 3) << 1) | (((row >> 1) & 1) ^ dx)
        column = pl.multiple_of(((chip << 1) | ((row & 1) ^ other)) * HD, HD)
        copies.append(
            pltpu.make_async_copy(
                pieces[piece].at[slot], relaid_ref.at[:, pl.ds(column, HD)], sems.at[k]
            )
        )
    start_and_wait(copies)


def place(me, pieces, slots, relaid):
    rows, width = pieces[0].shape[1:]
    first = relaid is None
    return call(
        functools.partial(place_kernel, len(pieces), slots),
        jax.ShapeDtypeStruct((rows, 16 * width), jnp.bfloat16),
        [SMEM] + [VMEM] * len(pieces) + ([] if first else [HBM]),
        HBM,
        [pltpu.SemaphoreType.DMA((len(slots),))],
        6,
        input_output_aliases={} if first else {len(pieces) + 1: 0},
    )(me, *pieces, *([] if first else [relaid]))


def body(
    tokens,
    norm_gain,
    query_weight,
    keyval_weight,
    out_weight,
    key_cache,
    value_cache,
    lengths,
    next_query,
):
    heads = query_weight.shape[1] // HD
    features = query_weight.shape[0] * lax.axis_size("row")
    me = jnp.stack([lax.axis_index("row"), lax.axis_index("col")]).astype(jnp.int32)
    cosine, sine = rotary_factors(lengths, HD)
    chunks = next_query.reshape(16, -1, next_query.shape[1])

    def pair(dy, dx):
        return [(dy, dx, 0), (dy, dx, 1)]

    to_a, to_b = stage(me, chunks, [pair(1, 0), pair(3, 0)])
    got_a, got_b = shift_y(to_a, 1), shift_y(to_b, 3)
    own, to_own, to_c, to_d, to_e, to_f, to_g = stage(
        me,
        chunks,
        [[(0, 0, 0)], [(0, 0, 1)], pair(2, 0), pair(0, 1), pair(1, 1), pair(3, 1), pair(2, 1)],
    )
    got_own = flip(to_own, "row", CORE)

    feats = tokens[None]
    other = flip(feats, "col", X_LOW)
    other, to_e, cosine, sine, to_c, to_d, to_f, to_g = tie(
        other, to_e, cosine, sine, to_c, to_d, to_f, to_g
    )
    via_e = flip(to_e, "row", X_HALF)
    feats = join(feats, other)
    other = flip(feats, "col", Z_NEAR)
    other, got_own = tie(other, got_own)
    feats = join(feats, other)
    other = flip(feats, "col", Z_FAR)
    got_c = shift_y(to_c, 2)
    kept, sent = project(me, feats, other, norm_gain, query_weight, keyval_weight)
    got_a, got_b, sent = tie(got_a, got_b, sent)
    got = flip(sent, "row", CORE)
    got, via_e = tie(got, via_e)
    kept, sent = add_halves(kept, got, 5)
    got = flip(sent, "row", X_HALF)
    via_f, via_g = flip(to_f, "row", X_HALF), flip(to_g, "row", X_HALF)
    got, got_c = tie(got, got_c)
    swap_first = flip(pack([got_a, got_b, got_c], [(k, 1) for k in range(3)]), "row", CORE)
    kept, sent = add_halves(kept, got, 10)
    got = flip(sent, "row", Y_FAR)
    kept, sent = add_halves(kept, got)
    got = flip(sent, "row", Y_NEAR)
    attended = attend(
        lengths, kept, got, cosine, sine, key_cache, value_cache, features, heads
    )
    other = flip(attended, "row", Y_NEAR)
    other, via_f = tie(other, via_f)
    attended = join(attended, other)
    other = flip(attended, "row", Y_FAR)
    got_e, got_f = shift_y(via_e, 1), shift_y(via_f, 3)
    via_g, swap_first, other = tie(via_g, swap_first, other)
    swap_g = flip(pack([via_g], [(0, 1)]), "row", CORE)
    attended = join(attended, other, 4.5)
    other = flip(attended, "row", X_HALF)
    got_d = flip(to_d, "row", X_HALF)
    attended = join(attended, other, 2.4)
    other = flip(attended, "row", CORE)
    relaid = place(
        me,
        [own, got_own, got_a, got_b, got_c, swap_first],
        [(0, 0, 0, 0, 0), (1, 0, 0, 0, 1)]
        + [(k + 2, 0, dy, 0, 0) for k, dy in enumerate((1, 3, 2))]
        + [(5, k, dy, 0, 1) for k, dy in enumerate((1, 3, 2))],
        None,
    )
    kept, sent = mix(me, attended, other, out_weight)
    via_g = pack([via_g, swap_g], [(0, 0), (1, 0)])
    got = flip(sent, "col", Z_FAR)
    got_g = shift_y(via_g, 2)
    got, got_e, got_f, relaid = tie(got, got_e, got_f, relaid)
    kept, sent = add_halves(kept, got, 3.2)
    got = flip(sent, "col", Z_NEAR)
    got, got_d = tie(got, got_d)
    swap_last = flip(pack([got_d, got_e, got_f], [(k, 1) for k in range(3)]), "row", CORE)
    kept, sent = add_halves(kept, got, 3.2)
    got = flip(sent, "col", X_LOW)
    mixed = (kept + got)[0].astype(jnp.bfloat16)
    relaid = place(
        me,
        [got_d, got_e, got_f, swap_last],
        [(k, 0, dy, 1, 0) for k, dy in enumerate((0, 1, 3))]
        + [(3, k, dy, 1, 1) for k, dy in enumerate((0, 1, 3))],
        relaid,
    )
    relaid = place(me, [got_g], [(0, 0, 2, 1, 0), (0, 1, 2, 1, 1)], relaid)
    return (mixed, relaid)


def solution(mesh):
    in_specs = (
        P(None, ("row", "col")),
        P("row"),
        P("row", "col"),
        P("row", "col"),
        P("col", "row"),
        P("row", None, "col"),
        P("row", None, "col"),
        P("row"),
        P(None, ("col", "row")),
    )
    out_specs = (P(None, ("row", "col")), P("row", "col"))
    return jax.shard_map(body, mesh=mesh, in_specs=in_specs, out_specs=out_specs, check_vma=False)
```

```python
import functools

import jax
import jax.numpy as jnp
from jax import lax
from jax.experimental import pallas as pl
from jax.experimental.pallas import tpu as pltpu
from jax.sharding import PartitionSpec as P

HD = 128
masked_score = -1e30
SQUARES = 128
CHUNK = 1024

CORE, X_HALF, Y_NEAR, Y_FAR = 1, 2, 4, 12
Z_NEAR, Z_FAR, X_LOW = 1, 2, 4

COST = 1_000_000_000
VMEM = pl.BlockSpec(memory_space=pltpu.VMEM)
SMEM = pl.BlockSpec(memory_space=pltpu.SMEM)
HBM = pl.BlockSpec(memory_space=pltpu.HBM)
ANYWHERE = pl.BlockSpec(memory_space=pl.ANY)


def call(kernel, out, in_specs, out_specs, scratch=(), megabytes=16, cost=0.0, **options):
    return pl.pallas_call(
        kernel,
        out_shape=out,
        in_specs=in_specs,
        out_specs=out_specs,
        scratch_shapes=list(scratch),
        compiler_params=pltpu.CompilerParams(vmem_limit_bytes=int(megabytes * 2**20)),
        cost_estimate=pl.CostEstimate(
            flops=int(cost * COST) + 1, bytes_accessed=1, transcendentals=0
        ),
        **options,
    )


def like(array, rows):
    return jax.ShapeDtypeStruct((rows,) + array.shape[1:], array.dtype)


def rotary_factors(positions, width):
    half_dim = width // 2
    freqs = 500000.0 ** (-(jnp.arange(half_dim).astype(jnp.float32) * 2.0 / width))
    angles = positions.astype(jnp.float32)[:, None] * freqs[None, :]
    cosine, sine = jnp.cos(angles), jnp.sin(angles)
    return (
        jnp.concatenate([cosine, cosine], axis=-1),
        jnp.concatenate([-sine, sine], axis=-1),
    )


def flip(block, axis, bits):
    size = lax.axis_size(axis)
    return lax.ppermute(block, axis, [(i, i ^ bits) for i in range(size)])


def shift_y(block, steps):
    size = lax.axis_size("row")
    return lax.ppermute(block, "row", [(i, (i + 4 * steps) % size) for i in range(size)])


def tie(*values):
    return lax.optimization_barrier(values)


def join_kernel(own_ref, other_ref, out_ref):
    rows = own_ref.shape[0]
    out_ref[:rows] = own_ref[...]
    out_ref[rows:] = other_ref[...]


def fetch_kernel(block_ref, out_ref, sem):
    copy = pltpu.make_async_copy(block_ref, out_ref, sem)
    copy.start()
    copy.wait()


def fetch(block):
    return call(
        fetch_kernel,
        like(block, block.shape[0]),
        [ANYWHERE],
        VMEM,
        [pltpu.SemaphoreType.DMA],
        megabytes=1,
    )(block)


def join(own, other, cost=0.0):
    both = like(own, 2 * own.shape[0])
    return call(join_kernel, both, [VMEM] * 2, VMEM, megabytes=2, cost=cost)(own, other)


def add_halves_kernel(kept_ref, got_ref, next_kept_ref, next_sent_ref):
    half = next_kept_ref.shape[0]
    next_kept_ref[...] = kept_ref[:half] + got_ref[:half]
    next_sent_ref[...] = kept_ref[half:] + got_ref[half:]


def add_halves(kept, got, cost=0.0):
    half = like(kept, kept.shape[0] // 2)
    return call(
        add_halves_kernel, [half, half], [VMEM] * 2, [VMEM] * 2, megabytes=2, cost=cost
    )(kept, got)


def gray(number):
    return number ^ (number >> 1)


def batch_row(me_ref, place):
    row = me_ref[0]
    y, x_half, core = row >> 2, (row >> 1) & 1, row & 1
    device = (
        ((y ^ gray((place >> 1) & 3)) << 2)
        | ((x_half ^ ((place >> 3) & 1)) << 1)
        | (core ^ (place >> 4))
    )
    return (device << 1) | (place & 1)


def project_kernel(
    me_ref, near_ref, far_ref, gain_ref, query_ref, keyval_ref, kept_ref, sent_ref, feats_scr
):
    half, rows = near_ref.shape[0], near_ref.shape[1]
    feats_scr[:half] = near_ref[...]
    feats_scr[half:] = far_ref[...]
    x_low, z = me_ref[1] >> 2, me_ref[1] & 3
    blocks = [
        feats_scr[((part & 3) ^ z) * 2 + ((part >> 2) ^ x_low)] for part in range(2 * half)
    ]
    shape = (rows, rows)
    order = batch_row(me_ref, lax.broadcasted_iota(jnp.int32, shape, 0))
    order = jnp.where(order == lax.broadcasted_iota(jnp.int32, shape, 1), 1.0, 0.0)
    feats = jnp.dot(
        order.astype(jnp.bfloat16),
        jnp.concatenate(blocks, axis=1),
        preferred_element_type=jnp.float32,
    )
    square_sum = jnp.sum(feats * feats, axis=1, keepdims=True)
    normed = (feats * gain_ref[...].astype(jnp.float32)).astype(jnp.bfloat16)
    columns = query_ref.shape[1]
    cut = rows // 2

    def put(start, values):
        end = start + values.shape[1]
        kept_ref[:, start:end] = values[:cut]
        sent_ref[:, start:end] = values[cut:]

    step = 512
    for start in range(0, columns, step):
        put(
            start,
            jnp.dot(
                normed, query_ref[:, start : start + step], preferred_element_type=jnp.float32
            ),
        )
    put(columns, jnp.dot(normed, keyval_ref[...], preferred_element_type=jnp.float32))
    put(columns + keyval_ref.shape[1], jnp.broadcast_to(square_sum, (rows, SQUARES)))


def project(me, near, far, gain, query_weight, keyval_weight):
    rows = near.shape[1]
    columns = query_weight.shape[1] + keyval_weight.shape[1] + SQUARES
    half = jax.ShapeDtypeStruct((rows // 2, columns), jnp.float32)
    return call(
        project_kernel,
        [half, half],
        [SMEM] + [VMEM] * 5,
        [VMEM] * 2,
        [pltpu.VMEM((2 * near.shape[0],) + near.shape[1:], near.dtype)],
    )(me, near, far, gain[None], query_weight, keyval_weight)


def attend_kernel(
    features, lengths_ref, kept_ref, got_ref, cos_ref, sin_ref, key_ref, value_ref, out_ref,
    proj_scr, query_scr, score_scr, rows_scr,
):
    rows, positions, head_dim = key_ref.shape
    heads = query_scr.shape[1]
    query_cols = heads * head_dim
    scale = head_dim ** (-0.5)
    proj_scr[...] = kept_ref[...] + got_ref[...]

    def rotate(vectors, b):
        return vectors * cos_ref[b : b + 1] + pltpu.roll(vectors, head_dim // 2, 1) * sin_ref[
            b : b + 1
        ]

    queries, tops, news = [], [], []
    for b in range(rows):
        squares = proj_scr[b : b + 1, -SQUARES:]
        inv_scale = lax.rsqrt(squares / features + 1e-05)
        for h in range(heads):
            query_scr[b, h : h + 1, :] = (
                proj_scr[b : b + 1, h * head_dim : (h + 1) * head_dim] * inv_scale
            )
        query = rotate(query_scr[b], b).astype(jnp.bfloat16)
        new_key = proj_scr[b : b + 1, query_cols : query_cols + head_dim] * inv_scale
        new_key = rotate(jnp.broadcast_to(new_key, (8, head_dim)), b)[:1].astype(jnp.bfloat16)
        new_value = proj_scr[b : b + 1, query_cols + head_dim : query_cols + 2 * head_dim]
        new_value = (new_value * inv_scale).astype(jnp.bfloat16).astype(jnp.float32)
        self_score = (
            jnp.sum(
                query.astype(jnp.float32) * new_key.astype(jnp.float32), axis=1, keepdims=True
            )
            * scale
        )
        queries.append(query)
        news.append((self_score, new_value))
        tops.append(jnp.full((heads, CHUNK), masked_score, jnp.float32))
    for start in range(0, positions, CHUNK):
        for b in range(rows):
            scores = (
                lax.dot_general(
                    queries[b],
                    key_ref[b, start : start + CHUNK, :],
                    (((1,), (1,)), ((), ())),
                    preferred_element_type=jnp.float32,
                )
                * scale
            )
            place = start + lax.broadcasted_iota(jnp.int32, scores.shape, 1)
            scores = jnp.where(place < lengths_ref[b], scores, masked_score)
            score_scr[b, :, start : start + CHUNK] = scores
            tops[b] = jnp.maximum(tops[b], scores)
    sums, numers = [], []
    for b, (self_score, new_value) in enumerate(news):
        tops[b] = jnp.maximum(jnp.max(tops[b], axis=1, keepdims=True), self_score)
        sums.append(jnp.zeros((heads, CHUNK), jnp.float32))
        numers.append(jnp.exp(self_score - tops[b]) * new_value)
    for start in range(0, positions, CHUNK):
        for b in range(rows):
            expos = jnp.exp(score_scr[b, :, start : start + CHUNK] - tops[b])
            sums[b] = sums[b] + expos
            numers[b] = numers[b] + jnp.dot(
                expos.astype(jnp.bfloat16),
                value_ref[b, start : start + CHUNK, :],
                preferred_element_type=jnp.float32,
            )
    for b, (self_score, new_value) in enumerate(news):
        totals = jnp.sum(sums[b], axis=1, keepdims=True) + jnp.exp(self_score - tops[b])
        attended = numers[b] / totals
        for h in range(heads):
            rows_scr[b : b + 1, h * head_dim : (h + 1) * head_dim] = attended[h : h + 1, :]
    out_ref[...] = rows_scr[...].astype(jnp.bfloat16)


def attend(lengths, kept, got, cosine, sine, key_cache, value_cache, features, heads):
    rows, positions, head_dim = key_cache.shape
    return call(
        functools.partial(attend_kernel, features),
        jax.ShapeDtypeStruct((rows, heads * head_dim), jnp.bfloat16),
        [SMEM] + [VMEM] * 6,
        VMEM,
        [
            pltpu.VMEM(kept.shape, jnp.float32),
            pltpu.VMEM((rows, heads, head_dim), jnp.float32),
            pltpu.VMEM((rows, heads, positions), jnp.float32),
            pltpu.VMEM((rows, heads * head_dim), jnp.float32),
        ],
    )(lengths, kept, got, cosine, sine, key_cache, value_cache)


def mix_kernel(me_ref, own_ref, other_ref, weight_ref, kept_ref, sent_ref, blocks_scr):
    rows = 2 * own_ref.shape[0]
    shape = (rows, rows)
    order = batch_row(me_ref, lax.broadcasted_iota(jnp.int32, shape, 1))
    order = jnp.where(order == lax.broadcasted_iota(jnp.int32, shape, 0), 1.0, 0.0)
    attended = jnp.dot(
        order.astype(jnp.bfloat16),
        jnp.concatenate([own_ref[...], other_ref[...]], axis=0),
        preferred_element_type=jnp.float32,
    ).astype(jnp.bfloat16)
    x_low, z = me_ref[1] >> 2, me_ref[1] & 3
    step, width = 256, kept_ref.shape[2]
    for start in range(0, weight_ref.shape[1], step):
        mixed = jnp.dot(
            attended, weight_ref[:, start : start + step], preferred_element_type=jnp.float32
        )
        for k in range(step // width):
            part = start // width + k
            place = ((part & 3) ^ z) * 2 + ((part >> 2) ^ x_low)
            blocks_scr[place] = mixed[:, k * width : (k + 1) * width]
    half = kept_ref.shape[0]
    kept_ref[...] = blocks_scr[:half]
    sent_ref[...] = blocks_scr[half:]


def mix(me, own, other, out_weight):
    rows, width = 2 * own.shape[0], out_weight.shape[1] // 8
    half = jax.ShapeDtypeStruct((4, rows, width), jnp.float32)
    return call(
        mix_kernel,
        [half, half],
        [SMEM] + [VMEM] * 3,
        [VMEM] * 2,
        [pltpu.VMEM((8, rows, width), jnp.float32)],
        cost=2.2,
    )(me, own, other, out_weight)


SAME, OTHER = "same", "other"


def pick(piece_ref, slot):
    if slot == SAME:
        return piece_ref.at[lax.axis_index("row") & 1]
    if slot == OTHER:
        return piece_ref.at[(lax.axis_index("row") & 1) ^ 1]
    return piece_ref.at[slot]


def start_and_wait(copies):
    for copy in copies:
        copy.start()
    for copy in copies:
        copy.wait()


def chip_pair(chunks, dy, dx):
    row = lax.axis_index("row")
    chip = ((((row >> 2) + dy) & 3) << 1) | (((row >> 1) & 1) ^ dx)
    return lax.dynamic_slice_in_dim(chunks, chip * 2, 2, 0)


def pack_kernel(count, slots, *refs):
    pieces, out_ref, sems = refs[:count], refs[-2], refs[-1]
    start_and_wait(
        [
            pltpu.make_async_copy(pick(pieces[p], i), out_ref.at[k], sems.at[k])
            for k, (p, i) in enumerate(slots)
        ]
    )


def pack(pieces, slots):
    return call(
        functools.partial(pack_kernel, len(pieces), slots),
        like(pieces[0], len(slots)),
        [ANYWHERE] * len(pieces),
        ANYWHERE,
        [pltpu.SemaphoreType.DMA((len(slots),))],
        1,
    )(*pieces)


def place_kernel(count, slots, me_ref, *refs):
    pieces, relaid_ref, sems = refs[:count], refs[-2], refs[-1]
    row = me_ref[0]
    copies = []
    for k, (piece, slot, dy, dx, other) in enumerate(slots):
        chip = ((((row >> 2) - dy) & 3) << 1) | (((row >> 1) & 1) ^ dx)
        column = pl.multiple_of(((chip << 1) | ((row & 1) ^ other)) * HD, HD)
        copies.append(
            pltpu.make_async_copy(
                pick(pieces[piece], slot), relaid_ref.at[:, pl.ds(column, HD)], sems.at[k]
            )
        )
    start_and_wait(copies)


def place(me, pieces, slots, relaid):
    rows, width = pieces[0].shape[1:]
    first = relaid is None
    return call(
        functools.partial(place_kernel, len(pieces), slots),
        jax.ShapeDtypeStruct((rows, 16 * width), jnp.bfloat16),
        [SMEM] + [VMEM] * len(pieces) + ([] if first else [HBM]),
        HBM,
        [pltpu.SemaphoreType.DMA((len(slots),))],
        6,
        input_output_aliases={} if first else {len(pieces) + 1: 0},
    )(me, *pieces, *([] if first else [relaid]))


def body(
    tokens,
    norm_gain,
    query_weight,
    keyval_weight,
    out_weight,
    key_cache,
    value_cache,
    lengths,
    next_query,
):
    heads = query_weight.shape[1] // HD
    features = query_weight.shape[0] * lax.axis_size("row")
    me = jnp.stack([lax.axis_index("row"), lax.axis_index("col")]).astype(jnp.int32)
    cosine, sine = rotary_factors(lengths, HD)
    chunks = next_query.reshape(16, -1, next_query.shape[1])

    def pair(dy, dx):
        return [(dy, dx, 0), (dy, dx, 1)]

    to_a, to_b, to_c, to_e = [chip_pair(chunks, *at) for at in ((1, 0), (3, 0), (2, 0), (1, 1))]
    got_a, got_b, got_c = shift_y(to_a, 1), shift_y(to_b, 3), shift_y(to_c, 2)

    other = flip(tokens[None], "col", X_LOW)
    feats = fetch(tokens[None])
    other, feats, to_e, cosine, sine = tie(other, feats, to_e, cosine, sine)
    via_e = flip(to_e, "row", X_HALF)
    feats = join(feats, other, 3)
    other = flip(feats, "col", Z_NEAR)
    other, chunks = tie(other, chunks)
    own, to_d, to_f, to_g = [chip_pair(chunks, *at) for at in ((0, 0), (0, 1), (3, 1), (2, 1))]
    feats = join(feats, other, 1.2)
    other = flip(feats, "col", Z_FAR)
    kept, sent = project(me, feats, other, norm_gain, query_weight, keyval_weight)
    got = flip(sent, "row", CORE)
    got, via_e, own, to_d, to_f, to_g = tie(got, via_e, own, to_d, to_f, to_g)
    kept, sent = add_halves(kept, got)
    got = flip(sent, "row", X_HALF)
    via_f = flip(to_f, "row", X_HALF)
    got, got_a, got_b, got_c = tie(got, got_a, got_b, got_c)
    swap_first = pack([own, got_a, got_b, got_c, to_d], [(k, OTHER) for k in range(5)])
    swap_first = flip(swap_first, "row", CORE)
    kept, sent = add_halves(kept, got, 8)
    got = flip(sent, "row", Y_FAR)
    via_g = flip(to_g, "row", X_HALF)
    swap_e = flip(pack([via_e], [(0, OTHER)]), "row", CORE)
    kept, sent = add_halves(kept, got, 3)
    got = flip(sent, "row", Y_NEAR)
    attended = attend(
        lengths, kept, got, cosine, sine, key_cache, value_cache, features, heads
    )
    other = flip(attended, "row", Y_NEAR)
    other, via_f, swap_e = tie(other, via_f, swap_e)
    via_e = pack([via_e, swap_e], [(0, SAME), (1, 0)])
    attended = join(attended, other, 3)
    other = flip(attended, "row", Y_FAR)
    got_e, got_f = shift_y(via_e, 1), shift_y(via_f, 3)
    via_g, swap_first, other = tie(via_g, swap_first, other)
    swap_g = flip(pack([via_g], [(0, OTHER)]), "row", CORE)
    attended = join(attended, other, 4.5)
    other = flip(attended, "row", X_HALF)
    got_d = flip(pack([to_d, swap_first], [(0, SAME), (1, 4)]), "row", X_HALF)
    attended = join(attended, other, 1.2)
    other = flip(attended, "row", CORE)
    relaid = place(
        me,
        [own, got_a, got_b, got_c, swap_first],
        [(k, SAME, dy, 0, 0) for k, dy in enumerate((0, 1, 3, 2))]
        + [(4, k, dy, 0, 1) for k, dy in enumerate((0, 1, 3, 2))],
        None,
    )
    kept, sent = mix(me, attended, other, out_weight)
    via_g = pack([via_g, swap_g], [(0, SAME), (1, 0)])
    got = flip(sent, "col", Z_FAR)
    got_g = shift_y(via_g, 2)
    got, got_e, got_f = tie(got, got_e, got_f)
    swap_last = flip(pack([got_f], [(0, OTHER)]), "row", CORE)
    kept, sent = add_halves(kept, got, 0.3)
    got = flip(sent, "col", Z_NEAR)
    got, got_d, relaid = tie(got, got_d, relaid)
    kept, sent = add_halves(kept, got)
    got = flip(sent, "col", X_LOW)
    relaid = place(
        me,
        [got_d, got_e, got_f],
        [(0, 0, 0, 1, 0), (1, 0, 1, 1, 0), (2, SAME, 3, 1, 0), (0, 1, 0, 1, 1), (1, 1, 1, 1, 1)],
        relaid,
    )
    got, relaid = tie(got, relaid)
    mixed = (kept + got)[0].astype(jnp.bfloat16)
    relaid = place(
        me,
        [got_g, swap_last],
        [(0, 0, 2, 1, 0), (0, 1, 2, 1, 1), (1, 0, 3, 1, 1)],
        relaid,
    )
    return (mixed, relaid)


def solution(mesh):
    in_specs = (
        P(None, ("row", "col")),
        P("row"),
        P("row", "col"),
        P("row", "col"),
        P("col", "row"),
        P("row", None, "col"),
        P("row", None, "col"),
        P("row"),
        P(None, ("col", "row")),
    )
    out_specs = (P(None, ("row", "col")), P("row", "col"))
    return jax.shard_map(body, mesh=mesh, in_specs=in_specs, out_specs=out_specs, check_vma=False)
```

```python
import functools

import jax
import jax.numpy as jnp
from jax import lax
from jax.experimental import pallas as pl
from jax.experimental.pallas import tpu as pltpu
from jax.sharding import PartitionSpec as P

HD = 128
masked_score = -1e30
SQUARES = 128
CHUNK = 1024

CORE, X_HALF, Y_NEAR, Y_FAR = 1, 2, 4, 12
Z_NEAR, Z_FAR, X_LOW = 1, 2, 4

COST = 1_000_000_000
VMEM = pl.BlockSpec(memory_space=pltpu.VMEM)
HBM = pl.BlockSpec(memory_space=pltpu.HBM)
ANYWHERE = pl.BlockSpec(memory_space=pl.ANY)


def call(kernel, out, in_specs, out_specs, scratch=(), megabytes=16, cost=0.0, **options):
    return pl.pallas_call(
        kernel,
        out_shape=out,
        in_specs=in_specs,
        out_specs=out_specs,
        scratch_shapes=list(scratch),
        compiler_params=pltpu.CompilerParams(vmem_limit_bytes=int(megabytes * 2**20)),
        cost_estimate=pl.CostEstimate(
            flops=int(cost * COST) + 1, bytes_accessed=1, transcendentals=0
        ),
        **options,
    )


def like(array, rows):
    return jax.ShapeDtypeStruct((rows,) + array.shape[1:], array.dtype)


def rotary_factors(positions, width):
    half_dim = width // 2
    freqs = 500000.0 ** (-(jnp.arange(half_dim).astype(jnp.float32) * 2.0 / width))
    angles = positions.astype(jnp.float32)[:, None] * freqs[None, :]
    cosine, sine = jnp.cos(angles), jnp.sin(angles)
    return (
        jnp.concatenate([cosine, cosine], axis=-1),
        jnp.concatenate([-sine, sine], axis=-1),
    )


def flip(block, axis, bits):
    size = lax.axis_size(axis)
    return lax.ppermute(block, axis, [(i, i ^ bits) for i in range(size)])


def shift_y(block, steps):
    size = lax.axis_size("row")
    return lax.ppermute(block, "row", [(i, (i + 4 * steps) % size) for i in range(size)])


def tie(*values):
    return lax.optimization_barrier(values)


def join_kernel(own_ref, other_ref, out_ref):
    rows = own_ref.shape[0]
    out_ref[:rows] = own_ref[...]
    out_ref[rows:] = other_ref[...]


def fetch_kernel(block_ref, out_ref, sem):
    copy = pltpu.make_async_copy(block_ref, out_ref, sem)
    copy.start()
    copy.wait()


def fetch(block):
    return call(
        fetch_kernel,
        like(block, block.shape[0]),
        [ANYWHERE],
        VMEM,
        [pltpu.SemaphoreType.DMA],
        megabytes=1,
    )(block)


def join(own, other, cost=0.0):
    both = like(own, 2 * own.shape[0])
    return call(join_kernel, both, [VMEM] * 2, VMEM, megabytes=2, cost=cost)(own, other)


def add_halves_kernel(kept_ref, got_ref, next_kept_ref, next_sent_ref):
    half = next_kept_ref.shape[0]
    next_kept_ref[...] = kept_ref[:half] + got_ref[:half]
    next_sent_ref[...] = kept_ref[half:] + got_ref[half:]


def add_halves(kept, got, cost=0.0):
    half = like(kept, kept.shape[0] // 2)
    return call(
        add_halves_kernel, [half, half], [VMEM] * 2, [VMEM] * 2, megabytes=2, cost=cost
    )(kept, got)


def gray(number):
    return number ^ (number >> 1)


def batch_row(place):
    row = lax.axis_index("row")
    y, x_half, core = row >> 2, (row >> 1) & 1, row & 1
    device = (
        ((y ^ gray((place >> 1) & 3)) << 2)
        | ((x_half ^ ((place >> 3) & 1)) << 1)
        | (core ^ (place >> 4))
    )
    return (device << 1) | (place & 1)


def project_kernel(
    near_ref, far_ref, gain_ref, query_ref, keyval_ref, kept_ref, sent_ref, feats_scr
):
    half, rows = near_ref.shape[0], near_ref.shape[1]
    feats_scr[:half] = near_ref[...]
    feats_scr[half:] = far_ref[...]
    x_low, z = lax.axis_index("col") >> 2, lax.axis_index("col") & 3
    blocks = [
        feats_scr[((part & 3) ^ z) * 2 + ((part >> 2) ^ x_low)] for part in range(2 * half)
    ]
    shape = (rows, rows)
    order = batch_row(lax.broadcasted_iota(jnp.int32, shape, 0))
    order = jnp.where(order == lax.broadcasted_iota(jnp.int32, shape, 1), 1.0, 0.0)
    feats = jnp.dot(
        order.astype(jnp.bfloat16),
        jnp.concatenate(blocks, axis=1),
        preferred_element_type=jnp.float32,
    )
    square_sum = jnp.sum(feats * feats, axis=1, keepdims=True)
    normed = (feats * gain_ref[...].astype(jnp.float32)).astype(jnp.bfloat16)
    columns = query_ref.shape[1]
    cut = rows // 2

    def put(start, values):
        end = start + values.shape[1]
        kept_ref[:, start:end] = values[:cut]
        sent_ref[:, start:end] = values[cut:]

    step = 512
    for start in range(0, columns, step):
        put(
            start,
            jnp.dot(
                normed, query_ref[:, start : start + step], preferred_element_type=jnp.float32
            ),
        )
    put(columns, jnp.dot(normed, keyval_ref[...], preferred_element_type=jnp.float32))
    put(columns + keyval_ref.shape[1], jnp.broadcast_to(square_sum, (rows, SQUARES)))


def project(near, far, gain, query_weight, keyval_weight):
    rows = near.shape[1]
    columns = query_weight.shape[1] + keyval_weight.shape[1] + SQUARES
    half = jax.ShapeDtypeStruct((rows // 2, columns), jnp.float32)
    return call(
        project_kernel,
        [half, half],
        [VMEM] * 5,
        [VMEM] * 2,
        [pltpu.VMEM((2 * near.shape[0],) + near.shape[1:], near.dtype)],
    )(near, far, gain[None], query_weight, keyval_weight)


def attend_kernel(
    features, lengths_ref, kept_ref, got_ref, cos_ref, sin_ref, key_ref, value_ref, out_ref,
    proj_scr, query_scr, score_scr, rows_scr,
):
    rows, positions, head_dim = key_ref.shape
    heads = query_scr.shape[1]
    query_cols = heads * head_dim
    scale = head_dim ** (-0.5)
    proj_scr[...] = kept_ref[...] + got_ref[...]

    def rotate(vectors, b):
        return vectors * cos_ref[b : b + 1] + pltpu.roll(vectors, head_dim // 2, 1) * sin_ref[
            b : b + 1
        ]

    queries, tops, news = [], [], []
    for b in range(rows):
        squares = proj_scr[b : b + 1, -SQUARES:]
        inv_scale = lax.rsqrt(squares / features + 1e-05)
        for h in range(heads):
            query_scr[b, h : h + 1, :] = (
                proj_scr[b : b + 1, h * head_dim : (h + 1) * head_dim] * inv_scale
            )
        query = rotate(query_scr[b], b).astype(jnp.bfloat16)
        new_key = proj_scr[b : b + 1, query_cols : query_cols + head_dim] * inv_scale
        new_key = rotate(jnp.broadcast_to(new_key, (8, head_dim)), b)[:1].astype(jnp.bfloat16)
        new_value = proj_scr[b : b + 1, query_cols + head_dim : query_cols + 2 * head_dim]
        new_value = (new_value * inv_scale).astype(jnp.bfloat16).astype(jnp.float32)
        self_score = (
            jnp.sum(
                query.astype(jnp.float32) * new_key.astype(jnp.float32), axis=1, keepdims=True
            )
            * scale
        )
        queries.append(query)
        news.append((self_score, new_value))
        tops.append(jnp.full((heads, CHUNK), masked_score, jnp.float32))
    for start in range(0, positions, CHUNK):
        for b in range(rows):
            scores = (
                lax.dot_general(
                    queries[b],
                    key_ref[b, start : start + CHUNK, :],
                    (((1,), (1,)), ((), ())),
                    preferred_element_type=jnp.float32,
                )
                * scale
            )
            place = start + lax.broadcasted_iota(jnp.int32, scores.shape, 1)
            scores = jnp.where(place < lengths_ref[b : b + 1, :1], scores, masked_score)
            score_scr[b, :, start : start + CHUNK] = scores
            tops[b] = jnp.maximum(tops[b], scores)
    sums, numers = [], []
    for b, (self_score, new_value) in enumerate(news):
        tops[b] = jnp.maximum(jnp.max(tops[b], axis=1, keepdims=True), self_score)
        sums.append(jnp.zeros((heads, CHUNK), jnp.float32))
        numers.append(jnp.exp(self_score - tops[b]) * new_value)
    for start in range(0, positions, CHUNK):
        for b in range(rows):
            expos = jnp.exp(score_scr[b, :, start : start + CHUNK] - tops[b])
            sums[b] = sums[b] + expos
            numers[b] = numers[b] + jnp.dot(
                expos.astype(jnp.bfloat16),
                value_ref[b, start : start + CHUNK, :],
                preferred_element_type=jnp.float32,
            )
    for b, (self_score, new_value) in enumerate(news):
        totals = jnp.sum(sums[b], axis=1, keepdims=True) + jnp.exp(self_score - tops[b])
        attended = numers[b] / totals
        for h in range(heads):
            rows_scr[b : b + 1, h * head_dim : (h + 1) * head_dim] = attended[h : h + 1, :]
    out_ref[...] = rows_scr[...].astype(jnp.bfloat16)


def attend(lengths, kept, got, cosine, sine, key_cache, value_cache, features, heads):
    rows, positions, head_dim = key_cache.shape
    return call(
        functools.partial(attend_kernel, features),
        jax.ShapeDtypeStruct((rows, heads * head_dim), jnp.bfloat16),
        [VMEM] * 7,
        VMEM,
        [
            pltpu.VMEM(kept.shape, jnp.float32),
            pltpu.VMEM((rows, heads, head_dim), jnp.float32),
            pltpu.VMEM((rows, heads, positions), jnp.float32),
            pltpu.VMEM((rows, heads * head_dim), jnp.float32),
        ],
        cost=2.2,
    )(lengths, kept, got, cosine, sine, key_cache, value_cache)


def mix_kernel(own_ref, other_ref, weight_ref, kept_ref, sent_ref, blocks_scr):
    rows = 2 * own_ref.shape[0]
    shape = (rows, rows)
    order = batch_row(lax.broadcasted_iota(jnp.int32, shape, 1))
    order = jnp.where(order == lax.broadcasted_iota(jnp.int32, shape, 0), 1.0, 0.0)
    attended = jnp.dot(
        order.astype(jnp.bfloat16),
        jnp.concatenate([own_ref[...], other_ref[...]], axis=0),
        preferred_element_type=jnp.float32,
    ).astype(jnp.bfloat16)
    step, width = 256, kept_ref.shape[2]
    for start in range(0, weight_ref.shape[1], step):
        mixed = jnp.dot(
            attended, weight_ref[:, start : start + step], preferred_element_type=jnp.float32
        )
        for k in range(step // width):
            blocks_scr[start // width + k] = mixed[:, k * width : (k + 1) * width]
    x_low, z = lax.axis_index("col") >> 2, lax.axis_index("col") & 3
    half = kept_ref.shape[0]
    for place in range(half):
        kept_ref[place] = blocks_scr[((x_low ^ (place & 1)) << 2) | (z ^ (place >> 1))]
        away = place + half
        sent_ref[place] = blocks_scr[((x_low ^ (away & 1)) << 2) | (z ^ (away >> 1))]


def mix(own, other, out_weight):
    rows, width = 2 * own.shape[0], out_weight.shape[1] // 8
    half = jax.ShapeDtypeStruct((4, rows, width), jnp.float32)
    return call(
        mix_kernel,
        [half, half],
        [VMEM] * 3,
        [VMEM] * 2,
        [pltpu.VMEM((8, rows, width), jnp.float32)],
        cost=2.2,
    )(own, other, out_weight)


SAME, OTHER = "same", "other"


def pick(piece_ref, slot, base=0):
    if slot == SAME:
        slot = lax.axis_index("row") & 1
    elif slot == OTHER:
        slot = (lax.axis_index("row") & 1) ^ 1
    return piece_ref.at[base + slot]


def start_and_wait(copies):
    for copy in copies:
        copy.start()
    for copy in copies:
        copy.wait()


def chip_pair(chunks, dy, dx):
    row = lax.axis_index("row")
    chip = ((((row >> 2) + dy) & 3) << 1) | (((row >> 1) & 1) ^ dx)
    return lax.dynamic_slice_in_dim(chunks, chip * 2, 2, 0)


def pack_kernel(count, slots, *refs):
    pieces, out_ref, sems = refs[:count], refs[-2], refs[-1]
    start_and_wait(
        [
            pltpu.make_async_copy(pick(pieces[p], *at), out_ref.at[k], sems.at[k])
            for k, (p, *at) in enumerate(slots)
        ]
    )


def pack(pieces, slots):
    return call(
        functools.partial(pack_kernel, len(pieces), slots),
        like(pieces[0], len(slots)),
        [ANYWHERE] * len(pieces),
        ANYWHERE,
        [pltpu.SemaphoreType.DMA((len(slots),))],
        1,
    )(*pieces)


def place_kernel(count, slots, *refs):
    pieces, relaid_ref, sems = refs[:count], refs[-2], refs[-1]
    row = lax.axis_index("row")
    copies = []
    for k, (piece, slot, dy, dx, other) in enumerate(slots):
        chip = ((((row >> 2) - dy) & 3) << 1) | (((row >> 1) & 1) ^ dx)
        column = pl.multiple_of(((chip << 1) | ((row & 1) ^ other)) * HD, HD)
        copies.append(
            pltpu.make_async_copy(
                pick(pieces[piece], slot), relaid_ref.at[:, pl.ds(column, HD)], sems.at[k]
            )
        )
    start_and_wait(copies)


def place(pieces, slots, relaid):
    rows, width = pieces[0].shape[1:]
    first = relaid is None
    return call(
        functools.partial(place_kernel, len(pieces), slots),
        jax.ShapeDtypeStruct((rows, 16 * width), jnp.bfloat16),
        [VMEM] * len(pieces) + ([] if first else [HBM]),
        HBM,
        [pltpu.SemaphoreType.DMA((len(slots),))],
        6,
        input_output_aliases={} if first else {len(pieces): 0},
    )(*pieces, *([] if first else [relaid]))


def body(
    tokens,
    norm_gain,
    query_weight,
    keyval_weight,
    out_weight,
    key_cache,
    value_cache,
    lengths,
    next_query,
):
    heads = query_weight.shape[1] // HD
    features = query_weight.shape[0] * lax.axis_size("row")
    cosine, sine = rotary_factors(lengths, HD)
    lengths = jnp.broadcast_to(lengths[:, None], cosine.shape)
    chunks = next_query.reshape(16, -1, next_query.shape[1])

    def pair(dy, dx):
        return [(dy, dx, 0), (dy, dx, 1)]

    to_a, to_b, to_c, to_e = [
        chip_pair(chunks, *at) for at in ((1, 0), (3, 0), (2, 0), (1, 1))
    ]
    got_a, got_b, got_c = shift_y(to_a, 1), shift_y(to_b, 3), shift_y(to_c, 2)

    other = flip(tokens[None], "col", X_LOW)
    feats = fetch(tokens[None])
    other, feats, to_e, cosine, sine, lengths = tie(other, feats, to_e, cosine, sine, lengths)
    via_e = flip(to_e, "row", X_HALF)
    feats = join(feats, other, 3)
    other = flip(feats, "col", Z_NEAR)
    other, chunks = tie(other, chunks)
    own, to_d, to_f, to_g = [chip_pair(chunks, *at) for at in ((0, 0), (0, 1), (3, 1), (2, 1))]
    feats = join(feats, other, 1.2)
    other = flip(feats, "col", Z_FAR)
    kept, sent = project(feats, other, norm_gain, query_weight, keyval_weight)
    got = flip(sent, "row", CORE)
    got, via_e, own, to_d, to_f, to_g = tie(got, via_e, own, to_d, to_f, to_g)
    kept, sent = add_halves(kept, got)
    got = flip(sent, "row", X_HALF)
    via_f = flip(to_f, "row", X_HALF)
    got, got_a, got_b, got_c = tie(got, got_a, got_b, got_c)
    swapped = pack(
        [own, got_a, got_b, got_c, to_d, via_e, to_g], [(k, OTHER) for k in range(7)]
    )
    swapped = flip(swapped, "row", CORE)
    kept, sent = add_halves(kept, got, 26)
    got = flip(sent, "row", Y_FAR)
    kept, sent = add_halves(kept, got)
    got = flip(sent, "row", Y_NEAR)
    via_g = flip(pack([to_g, swapped], [(0, SAME), (1, 6)]), "row", X_HALF)
    attended = attend(
        lengths, kept, got, cosine, sine, key_cache, value_cache, features, heads
    )
    other = flip(attended, "row", Y_NEAR)
    other, via_f = tie(other, via_f)
    via_e = pack([via_e, swapped], [(0, SAME), (1, 5)])
    attended = join(attended, other, 3)
    other = flip(attended, "row", Y_FAR)
    got_e, got_f = shift_y(via_e, 1), shift_y(via_f, 3)
    via_g, other = tie(via_g, other)
    attended = join(attended, other, 4.5)
    other = flip(attended, "row", X_HALF)
    got_d = flip(pack([to_d, swapped], [(0, SAME), (1, 4)]), "row", X_HALF)
    attended = join(attended, other, 1.2)
    other = flip(attended, "row", CORE)
    relaid = place(
        [own, got_a, got_b, got_c, swapped],
        [(k, SAME, dy, 0, 0) for k, dy in enumerate((0, 1, 3, 2))]
        + [(4, k, dy, 0, 1) for k, dy in enumerate((0, 1, 3, 2))],
        None,
    )
    kept, sent = mix(attended, other, out_weight)
    got = flip(sent, "col", Z_FAR)
    got_g = shift_y(via_g, 2)
    got, got_e, got_f = tie(got, got_e, got_f)
    swap_last = flip(pack([got_f], [(0, OTHER)]), "row", CORE)
    kept, sent = add_halves(kept, got, 0.3)
    got = flip(sent, "col", Z_NEAR)
    got, got_d, relaid = tie(got, got_d, relaid)
    kept, sent = add_halves(kept, got)
    got = flip(sent, "col", X_LOW)
    relaid = place(
        [got_d, got_e, got_f],
        [(0, 0, 0, 1, 0), (1, 0, 1, 1, 0), (2, SAME, 3, 1, 0), (0, 1, 0, 1, 1), (1, 1, 1, 1, 1)],
        relaid,
    )
    got, relaid = tie(got, relaid)
    mixed = (kept + got)[0].astype(jnp.bfloat16)
    relaid = place(
        [got_g, swap_last],
        [(0, 0, 2, 1, 0), (0, 1, 2, 1, 1), (1, 0, 3, 1, 1)],
        relaid,
    )
    return (mixed, relaid)


def solution(mesh):
    in_specs = (
        P(None, ("row", "col")),
        P("row"),
        P("row", "col"),
        P("row", "col"),
        P("col", "row"),
        P("row", None, "col"),
        P("row", None, "col"),
        P("row"),
        P(None, ("col", "row")),
    )
    out_specs = (P(None, ("row", "col")), P("row", "col"))
    return jax.shard_map(body, mesh=mesh, in_specs=in_specs, out_specs=out_specs, check_vma=False)
```

```python
import functools

import jax
import jax.numpy as jnp
from jax import lax
from jax.experimental import pallas as pl
from jax.experimental.pallas import tpu as pltpu
from jax.sharding import PartitionSpec as P

HD = 128
masked_score = -1e30
SQUARES = 128
CHUNK = 1024

CORE, X_HALF, Y_NEAR, Y_FAR = 1, 2, 4, 12
Z_NEAR, Z_FAR, X_LOW = 1, 2, 4

COST = 1_000_000_000
VMEM = pl.BlockSpec(memory_space=pltpu.VMEM)
HBM = pl.BlockSpec(memory_space=pltpu.HBM)
ANYWHERE = pl.BlockSpec(memory_space=pl.ANY)


def call(kernel, out, in_specs, out_specs, scratch=(), megabytes=16, cost=0.0, **options):
    return pl.pallas_call(
        kernel,
        out_shape=out,
        in_specs=in_specs,
        out_specs=out_specs,
        scratch_shapes=list(scratch),
        compiler_params=pltpu.CompilerParams(vmem_limit_bytes=int(megabytes * 2**20)),
        cost_estimate=pl.CostEstimate(
            flops=int(cost * COST) + 1, bytes_accessed=1, transcendentals=0
        ),
        **options,
    )


def like(array, rows):
    return jax.ShapeDtypeStruct((rows,) + array.shape[1:], array.dtype)


def rotary_factors(positions, width):
    half_dim = width // 2
    freqs = 500000.0 ** (-(jnp.arange(half_dim).astype(jnp.float32) * 2.0 / width))
    angles = positions.astype(jnp.float32)[:, None] * freqs[None, :]
    cosine, sine = jnp.cos(angles), jnp.sin(angles)
    return (
        jnp.concatenate([cosine, cosine], axis=-1),
        jnp.concatenate([-sine, sine], axis=-1),
    )


def flip(block, axis, bits):
    size = lax.axis_size(axis)
    return lax.ppermute(block, axis, [(i, i ^ bits) for i in range(size)])


def shift_y(block, steps):
    size = lax.axis_size("row")
    return lax.ppermute(block, "row", [(i, (i + 4 * steps) % size) for i in range(size)])


def tie(*values):
    return lax.optimization_barrier(values)


def join_kernel(own_ref, other_ref, out_ref):
    rows = own_ref.shape[0]
    out_ref[:rows] = own_ref[...]
    out_ref[rows:] = other_ref[...]


def fetch_kernel(block_ref, out_ref, sem):
    copy = pltpu.make_async_copy(block_ref, out_ref, sem)
    copy.start()
    copy.wait()


def fetch(block):
    return call(
        fetch_kernel,
        like(block, block.shape[0]),
        [ANYWHERE],
        VMEM,
        [pltpu.SemaphoreType.DMA],
        megabytes=1,
    )(block)


def join(own, other, cost=0.0):
    both = like(own, 2 * own.shape[0])
    return call(join_kernel, both, [VMEM] * 2, VMEM, megabytes=2, cost=cost)(own, other)


def add_halves_kernel(kept_ref, got_ref, next_kept_ref, next_sent_ref):
    half = next_kept_ref.shape[0]
    next_kept_ref[...] = kept_ref[:half] + got_ref[:half]
    next_sent_ref[...] = kept_ref[half:] + got_ref[half:]


def add_halves(kept, got, cost=0.0):
    half = like(kept, kept.shape[0] // 2)
    return call(
        add_halves_kernel, [half, half], [VMEM] * 2, [VMEM] * 2, megabytes=2, cost=cost
    )(kept, got)


def gray(number):
    return number ^ (number >> 1)


def batch_row(place):
    row = lax.axis_index("row")
    y, x_half, core = row >> 2, (row >> 1) & 1, row & 1
    device = (
        ((y ^ gray((place >> 1) & 3)) << 2)
        | ((x_half ^ ((place >> 3) & 1)) << 1)
        | (core ^ (place >> 4))
    )
    return (device << 1) | (place & 1)


def project_kernel(
    near_ref, far_ref, gain_ref, query_ref, keyval_ref, kept_ref, sent_ref, feats_scr
):
    half, rows = near_ref.shape[0], near_ref.shape[1]
    feats_scr[:half] = near_ref[...]
    feats_scr[half:] = far_ref[...]
    x_low, z = lax.axis_index("col") >> 2, lax.axis_index("col") & 3
    blocks = [
        feats_scr[((part & 3) ^ z) * 2 + ((part >> 2) ^ x_low)] for part in range(2 * half)
    ]
    shape = (rows, rows)
    order = batch_row(lax.broadcasted_iota(jnp.int32, shape, 0))
    order = jnp.where(order == lax.broadcasted_iota(jnp.int32, shape, 1), 1.0, 0.0)
    feats = jnp.dot(
        order.astype(jnp.bfloat16),
        jnp.concatenate(blocks, axis=1),
        preferred_element_type=jnp.float32,
    )
    square_sum = jnp.sum(feats * feats, axis=1, keepdims=True)
    normed = (feats * gain_ref[...].astype(jnp.float32)).astype(jnp.bfloat16)
    columns = query_ref.shape[1]
    cut = rows // 2

    def put(start, values):
        end = start + values.shape[1]
        kept_ref[:, start:end] = values[:cut]
        sent_ref[:, start:end] = values[cut:]

    step = 512
    for start in range(0, columns, step):
        put(
            start,
            jnp.dot(
                normed, query_ref[:, start : start + step], preferred_element_type=jnp.float32
            ),
        )
    put(columns, jnp.dot(normed, keyval_ref[...], preferred_element_type=jnp.float32))
    put(columns + keyval_ref.shape[1], jnp.broadcast_to(square_sum, (rows, SQUARES)))


def project(near, far, gain, query_weight, keyval_weight):
    rows = near.shape[1]
    columns = query_weight.shape[1] + keyval_weight.shape[1] + SQUARES
    half = jax.ShapeDtypeStruct((rows // 2, columns), jnp.float32)
    return call(
        project_kernel,
        [half, half],
        [VMEM] * 5,
        [VMEM] * 2,
        [pltpu.VMEM((2 * near.shape[0],) + near.shape[1:], near.dtype)],
    )(near, far, gain[None], query_weight, keyval_weight)


def attend_kernel(
    features, lengths_ref, kept_ref, got_ref, cos_ref, sin_ref, key_ref, value_ref, out_ref,
    proj_scr, query_scr, score_scr, rows_scr,
):
    rows, positions, head_dim = key_ref.shape
    heads = query_scr.shape[1]
    query_cols = heads * head_dim
    scale = head_dim ** (-0.5)
    proj_scr[...] = kept_ref[...] + got_ref[...]

    def rotate(vectors, b):
        return vectors * cos_ref[b : b + 1] + pltpu.roll(vectors, head_dim // 2, 1) * sin_ref[
            b : b + 1
        ]

    queries, tops, news = [], [], []
    for b in range(rows):
        squares = proj_scr[b : b + 1, -SQUARES:]
        inv_scale = lax.rsqrt(squares / features + 1e-05)
        for h in range(heads):
            query_scr[b, h : h + 1, :] = (
                proj_scr[b : b + 1, h * head_dim : (h + 1) * head_dim] * inv_scale
            )
        query = rotate(query_scr[b], b).astype(jnp.bfloat16)
        new_key = proj_scr[b : b + 1, query_cols : query_cols + head_dim] * inv_scale
        new_key = rotate(jnp.broadcast_to(new_key, (8, head_dim)), b)[:1].astype(jnp.bfloat16)
        new_value = proj_scr[b : b + 1, query_cols + head_dim : query_cols + 2 * head_dim]
        new_value = (new_value * inv_scale).astype(jnp.bfloat16).astype(jnp.float32)
        self_score = (
            jnp.sum(
                query.astype(jnp.float32) * new_key.astype(jnp.float32), axis=1, keepdims=True
            )
            * scale
        )
        queries.append(query)
        news.append((self_score, new_value))
        tops.append(jnp.full((heads, CHUNK), masked_score, jnp.float32))
    for start in range(0, positions, CHUNK):
        for b in range(rows):
            scores = (
                lax.dot_general(
                    queries[b],
                    key_ref[b, start : start + CHUNK, :],
                    (((1,), (1,)), ((), ())),
                    preferred_element_type=jnp.float32,
                )
                * scale
            )
            place = start + lax.broadcasted_iota(jnp.int32, scores.shape, 1)
            scores = jnp.where(place < lengths_ref[b : b + 1, :1], scores, masked_score)
            score_scr[b, :, start : start + CHUNK] = scores
            tops[b] = jnp.maximum(tops[b], scores)
    sums, numers = [], []
    for b, (self_score, new_value) in enumerate(news):
        tops[b] = jnp.maximum(jnp.max(tops[b], axis=1, keepdims=True), self_score)
        sums.append(jnp.zeros((heads, CHUNK), jnp.float32))
        numers.append(jnp.exp(self_score - tops[b]) * new_value)
    for start in range(0, positions, CHUNK):
        for b in range(rows):
            expos = jnp.exp(score_scr[b, :, start : start + CHUNK] - tops[b])
            sums[b] = sums[b] + expos
            numers[b] = numers[b] + jnp.dot(
                expos.astype(jnp.bfloat16),
                value_ref[b, start : start + CHUNK, :],
                preferred_element_type=jnp.float32,
            )
    for b, (self_score, new_value) in enumerate(news):
        totals = jnp.sum(sums[b], axis=1, keepdims=True) + jnp.exp(self_score - tops[b])
        attended = numers[b] / totals
        for h in range(heads):
            rows_scr[b : b + 1, h * head_dim : (h + 1) * head_dim] = attended[h : h + 1, :]
    out_ref[...] = rows_scr[...].astype(jnp.bfloat16)


def attend(lengths, kept, got, cosine, sine, key_cache, value_cache, features, heads):
    rows, positions, head_dim = key_cache.shape
    return call(
        functools.partial(attend_kernel, features),
        jax.ShapeDtypeStruct((rows, heads * head_dim), jnp.bfloat16),
        [VMEM] * 7,
        VMEM,
        [
            pltpu.VMEM(kept.shape, jnp.float32),
            pltpu.VMEM((rows, heads, head_dim), jnp.float32),
            pltpu.VMEM((rows, heads, positions), jnp.float32),
            pltpu.VMEM((rows, heads * head_dim), jnp.float32),
        ],
        cost=2.2,
    )(lengths, kept, got, cosine, sine, key_cache, value_cache)


def mix_kernel(own_ref, other_ref, weight_ref, kept_ref, sent_ref, blocks_scr):
    rows = 2 * own_ref.shape[0]
    shape = (rows, rows)
    order = batch_row(lax.broadcasted_iota(jnp.int32, shape, 1))
    order = jnp.where(order == lax.broadcasted_iota(jnp.int32, shape, 0), 1.0, 0.0)
    attended = jnp.dot(
        order.astype(jnp.bfloat16),
        jnp.concatenate([own_ref[...], other_ref[...]], axis=0),
        preferred_element_type=jnp.float32,
    ).astype(jnp.bfloat16)
    step, width = 256, kept_ref.shape[2]
    for start in range(0, weight_ref.shape[1], step):
        mixed = jnp.dot(
            attended, weight_ref[:, start : start + step], preferred_element_type=jnp.float32
        )
        for k in range(step // width):
            blocks_scr[start // width + k] = mixed[:, k * width : (k + 1) * width]
    x_low, z = lax.axis_index("col") >> 2, lax.axis_index("col") & 3
    half = kept_ref.shape[0]
    for place in range(half):
        kept_ref[place] = blocks_scr[((x_low ^ (place & 1)) << 2) | (z ^ (place >> 1))]
        away = place + half
        sent_ref[place] = blocks_scr[((x_low ^ (away & 1)) << 2) | (z ^ (away >> 1))]


def mix(own, other, out_weight):
    rows, width = 2 * own.shape[0], out_weight.shape[1] // 8
    half = jax.ShapeDtypeStruct((4, rows, width), jnp.float32)
    return call(
        mix_kernel,
        [half, half],
        [VMEM] * 3,
        [VMEM] * 2,
        [pltpu.VMEM((8, rows, width), jnp.float32)],
        cost=2.2,
    )(own, other, out_weight)


SAME, OTHER = "same", "other"


def pick(piece_ref, slot, base=0):
    if slot == SAME:
        slot = lax.axis_index("row") & 1
    elif slot == OTHER:
        slot = (lax.axis_index("row") & 1) ^ 1
    return piece_ref.at[base + slot]


def start_and_wait(copies):
    for copy in copies:
        copy.start()
    for copy in copies:
        copy.wait()


def chip_pair(chunks, dy, dx):
    row = lax.axis_index("row")
    chip = ((((row >> 2) + dy) & 3) << 1) | (((row >> 1) & 1) ^ dx)
    return lax.dynamic_slice_in_dim(chunks, chip * 2, 2, 0)


def stage_kernel(groups, chunks_ref, *refs):
    pieces, (buffer, in_sems, out_sems) = refs[: len(groups)], refs[len(groups) :]
    row = lax.axis_index("row")
    copies = []
    for piece, group in zip(pieces, groups):
        for i, (dy, dx, core) in enumerate(group):
            chip = ((((row >> 2) + dy) & 3) << 1) | (((row >> 1) & 1) ^ dx)
            k = len(copies)
            copies.append(
                (
                    pltpu.make_async_copy(
                        chunks_ref.at[(chip << 1) | core], buffer.at[k], in_sems.at[k]
                    ),
                    pltpu.make_async_copy(buffer.at[k], piece.at[i], out_sems.at[k]),
                )
            )
    for fetch, _ in copies:
        fetch.start()
    for fetch, store in copies:
        fetch.wait()
        store.start()
    for _, store in copies:
        store.wait()


def stage(chunks, groups):
    count = sum(len(group) for group in groups)
    return call(
        functools.partial(stage_kernel, groups),
        [like(chunks, len(group)) for group in groups],
        [HBM],
        [HBM] * len(groups),
        [
            pltpu.VMEM((count,) + chunks.shape[1:], chunks.dtype),
            pltpu.SemaphoreType.DMA((count,)),
            pltpu.SemaphoreType.DMA((count,)),
        ],
        60,
    )(chunks)


def pack_kernel(count, slots, *refs):
    pieces, out_ref, sems = refs[:count], refs[-2], refs[-1]
    start_and_wait(
        [
            pltpu.make_async_copy(pick(pieces[p], *at), out_ref.at[k], sems.at[k])
            for k, (p, *at) in enumerate(slots)
        ]
    )


def pack(pieces, slots):
    return call(
        functools.partial(pack_kernel, len(pieces), slots),
        like(pieces[0], len(slots)),
        [ANYWHERE] * len(pieces),
        ANYWHERE,
        [pltpu.SemaphoreType.DMA((len(slots),))],
        1,
    )(*pieces)


def place_kernel(count, slots, *refs):
    pieces, relaid_ref, sems = refs[:count], refs[-2], refs[-1]
    row = lax.axis_index("row")
    copies = []
    for k, (piece, slot, dy, dx, other) in enumerate(slots):
        chip = ((((row >> 2) - dy) & 3) << 1) | (((row >> 1) & 1) ^ dx)
        column = pl.multiple_of(((chip << 1) | ((row & 1) ^ other)) * HD, HD)
        copies.append(
            pltpu.make_async_copy(
                pick(pieces[piece], slot), relaid_ref.at[:, pl.ds(column, HD)], sems.at[k]
            )
        )
    start_and_wait(copies)


def place(pieces, slots, relaid):
    rows, width = pieces[0].shape[1:]
    first = relaid is None
    return call(
        functools.partial(place_kernel, len(pieces), slots),
        jax.ShapeDtypeStruct((rows, 16 * width), jnp.bfloat16),
        [VMEM] * len(pieces) + ([] if first else [HBM]),
        HBM,
        [pltpu.SemaphoreType.DMA((len(slots),))],
        6,
        input_output_aliases={} if first else {len(pieces): 0},
    )(*pieces, *([] if first else [relaid]))


def body(
    tokens,
    norm_gain,
    query_weight,
    keyval_weight,
    out_weight,
    key_cache,
    value_cache,
    lengths,
    next_query,
):
    heads = query_weight.shape[1] // HD
    features = query_weight.shape[0] * lax.axis_size("row")
    cosine, sine = rotary_factors(lengths, HD)
    lengths = jnp.broadcast_to(lengths[:, None], cosine.shape)
    chunks = next_query.reshape(16, -1, next_query.shape[1])

    def pair(dy, dx):
        return [(dy, dx, 0), (dy, dx, 1)]

    to_a, to_b, to_c, to_e = stage(
        chunks,
        [
            [(dy, dx, core) for core in range(2)]
            for dy, dx in ((1, 0), (3, 0), (2, 0), (1, 1))
        ],
    )
    got_a, got_b, got_c = shift_y(to_a, 1), shift_y(to_b, 3), shift_y(to_c, 2)

    other = flip(tokens[None], "col", X_LOW)
    feats = fetch(tokens[None])
    other, feats, to_e, cosine, sine, lengths = tie(other, feats, to_e, cosine, sine, lengths)
    via_e = flip(to_e, "row", X_HALF)
    feats = join(feats, other, 3)
    other = flip(feats, "col", Z_NEAR)
    other, chunks = tie(other, chunks)
    own, to_d, to_f, to_g = [chip_pair(chunks, *at) for at in ((0, 0), (0, 1), (3, 1), (2, 1))]
    feats = join(feats, other, 1.2)
    other = flip(feats, "col", Z_FAR)
    kept, sent = project(feats, other, norm_gain, query_weight, keyval_weight)
    got = flip(sent, "row", CORE)
    got, via_e, own, to_d, to_f, to_g = tie(got, via_e, own, to_d, to_f, to_g)
    kept, sent = add_halves(kept, got)
    got = flip(sent, "row", X_HALF)
    via_f = flip(to_f, "row", X_HALF)
    got, got_a, got_b, got_c = tie(got, got_a, got_b, got_c)
    swapped = pack(
        [own, got_a, got_b, got_c, to_d, via_e, to_g], [(k, OTHER) for k in range(7)]
    )
    swapped = flip(swapped, "row", CORE)
    kept, sent = add_halves(kept, got, 26)
    got = flip(sent, "row", Y_FAR)
    kept, sent = add_halves(kept, got)
    got = flip(sent, "row", Y_NEAR)
    via_g = flip(pack([to_g, swapped], [(0, SAME), (1, 6)]), "row", X_HALF)
    attended = attend(
        lengths, kept, got, cosine, sine, key_cache, value_cache, features, heads
    )
    other = flip(attended, "row", Y_NEAR)
    other, via_f = tie(other, via_f)
    via_e = pack([via_e, swapped], [(0, SAME), (1, 5)])
    attended = join(attended, other, 3)
    other = flip(attended, "row", Y_FAR)
    got_e, got_f = shift_y(via_e, 1), shift_y(via_f, 3)
    via_g, other = tie(via_g, other)
    attended = join(attended, other, 4.5)
    other = flip(attended, "row", X_HALF)
    got_d = flip(pack([to_d, swapped], [(0, SAME), (1, 4)]), "row", X_HALF)
    attended = join(attended, other, 1.2)
    other = flip(attended, "row", CORE)
    relaid = place(
        [own, got_a, got_b, got_c, swapped],
        [(k, SAME, dy, 0, 0) for k, dy in enumerate((0, 1, 3, 2))]
        + [(4, k, dy, 0, 1) for k, dy in enumerate((0, 1, 3, 2))],
        None,
    )
    kept, sent = mix(attended, other, out_weight)
    got = flip(sent, "col", Z_FAR)
    got_g = shift_y(via_g, 2)
    got, got_e, got_f = tie(got, got_e, got_f)
    swap_last = flip(pack([got_f], [(0, OTHER)]), "row", CORE)
    kept, sent = add_halves(kept, got, 0.3)
    got = flip(sent, "col", Z_NEAR)
    got, got_d, relaid = tie(got, got_d, relaid)
    kept, sent = add_halves(kept, got)
    got = flip(sent, "col", X_LOW)
    relaid = place(
        [got_d, got_e, got_f],
        [(0, 0, 0, 1, 0), (1, 0, 1, 1, 0), (2, SAME, 3, 1, 0), (0, 1, 0, 1, 1), (1, 1, 1, 1, 1)],
        relaid,
    )
    got, relaid = tie(got, relaid)
    mixed = (kept + got)[0].astype(jnp.bfloat16)
    relaid = place(
        [got_g, swap_last],
        [(0, 0, 2, 1, 0), (0, 1, 2, 1, 1), (1, 0, 3, 1, 1)],
        relaid,
    )
    return (mixed, relaid)


def solution(mesh):
    in_specs = (
        P(None, ("row", "col")),
        P("row"),
        P("row", "col"),
        P("row", "col"),
        P("col", "row"),
        P("row", None, "col"),
        P("row", None, "col"),
        P("row"),
        P(None, ("col", "row")),
    )
    out_specs = (P(None, ("row", "col")), P("row", "col"))
    return jax.shard_map(body, mesh=mesh, in_specs=in_specs, out_specs=out_specs, check_vma=False)
```

```python
import functools

import jax
import jax.numpy as jnp
from jax import lax
from jax.experimental import pallas as pl
from jax.experimental.pallas import tpu as pltpu
from jax.sharding import PartitionSpec as P

HD = 128
masked_score = -1e30
SQUARES = 128
CHUNK = 1024

CORE, X_HALF, Y_NEAR, Y_FAR = 1, 2, 4, 12
Z_NEAR, Z_FAR, X_LOW = 1, 2, 4

COST = 1_000_000_000
VMEM = pl.BlockSpec(memory_space=pltpu.VMEM)
HBM = pl.BlockSpec(memory_space=pltpu.HBM)
ANYWHERE = pl.BlockSpec(memory_space=pl.ANY)


def call(kernel, out, in_specs, out_specs, scratch=(), megabytes=16, cost=0.0, **options):
    return pl.pallas_call(
        kernel,
        out_shape=out,
        in_specs=in_specs,
        out_specs=out_specs,
        scratch_shapes=list(scratch),
        compiler_params=pltpu.CompilerParams(vmem_limit_bytes=int(megabytes * 2**20)),
        cost_estimate=pl.CostEstimate(
            flops=int(cost * COST) + 1, bytes_accessed=1, transcendentals=0
        ),
        **options,
    )


def like(array, rows):
    return jax.ShapeDtypeStruct((rows,) + array.shape[1:], array.dtype)


def rotary_factors(positions, width):
    half_dim = width // 2
    freqs = 500000.0 ** (-(jnp.arange(half_dim).astype(jnp.float32) * 2.0 / width))
    angles = positions.astype(jnp.float32)[:, None] * freqs[None, :]
    cosine, sine = jnp.cos(angles), jnp.sin(angles)
    return (
        jnp.concatenate([cosine, cosine], axis=-1),
        jnp.concatenate([-sine, sine], axis=-1),
    )


def flip(block, axis, bits):
    size = lax.axis_size(axis)
    return lax.ppermute(block, axis, [(i, i ^ bits) for i in range(size)])


def shift_y(block, steps):
    size = lax.axis_size("row")
    return lax.ppermute(block, "row", [(i, (i + 4 * steps) % size) for i in range(size)])


def tie(*values):
    return lax.optimization_barrier(values)


def join_kernel(own_ref, other_ref, out_ref):
    rows = own_ref.shape[0]
    out_ref[:rows] = own_ref[...]
    out_ref[rows:] = other_ref[...]


def fetch_kernel(block_ref, out_ref, sem):
    copy = pltpu.make_async_copy(block_ref, out_ref, sem)
    copy.start()
    copy.wait()


def fetch(block):
    return call(
        fetch_kernel,
        like(block, block.shape[0]),
        [ANYWHERE],
        VMEM,
        [pltpu.SemaphoreType.DMA],
        megabytes=1,
    )(block)


def join(own, other, cost=0.0):
    both = like(own, 2 * own.shape[0])
    return call(join_kernel, both, [VMEM] * 2, VMEM, megabytes=2, cost=cost)(own, other)


def add_halves_kernel(kept_ref, got_ref, next_kept_ref, next_sent_ref):
    half = next_kept_ref.shape[0]
    next_kept_ref[...] = kept_ref[:half] + got_ref[:half]
    next_sent_ref[...] = kept_ref[half:] + got_ref[half:]


def add_halves(kept, got, cost=0.0):
    half = like(kept, kept.shape[0] // 2)
    return call(
        add_halves_kernel, [half, half], [VMEM] * 2, [VMEM] * 2, megabytes=2, cost=cost
    )(kept, got)


def gray(number):
    return number ^ (number >> 1)


def batch_row(place):
    row = lax.axis_index("row")
    y, x_half, core = row >> 2, (row >> 1) & 1, row & 1
    device = (
        ((y ^ gray((place >> 1) & 3)) << 2)
        | ((x_half ^ ((place >> 3) & 1)) << 1)
        | (core ^ (place >> 4))
    )
    return (device << 1) | (place & 1)


def project_kernel(
    near_ref, far_ref, gain_ref, query_ref, keyval_ref, kept_ref, sent_ref, feats_scr
):
    half, rows = near_ref.shape[0], near_ref.shape[1]
    feats_scr[:half] = near_ref[...]
    feats_scr[half:] = far_ref[...]
    x_low, z = lax.axis_index("col") >> 2, lax.axis_index("col") & 3
    blocks = [
        feats_scr[((part & 3) ^ z) * 2 + ((part >> 2) ^ x_low)] for part in range(2 * half)
    ]
    shape = (rows, rows)
    order = batch_row(lax.broadcasted_iota(jnp.int32, shape, 0))
    order = jnp.where(order == lax.broadcasted_iota(jnp.int32, shape, 1), 1.0, 0.0)
    feats = jnp.dot(
        order.astype(jnp.bfloat16),
        jnp.concatenate(blocks, axis=1),
        preferred_element_type=jnp.float32,
    )
    square_sum = jnp.sum(feats * feats, axis=1, keepdims=True)
    normed = (feats * gain_ref[...].astype(jnp.float32)).astype(jnp.bfloat16)
    columns = query_ref.shape[1]
    cut = rows // 2

    def put(start, values):
        end = start + values.shape[1]
        kept_ref[:, start:end] = values[:cut]
        sent_ref[:, start:end] = values[cut:]

    step = 512
    for start in range(0, columns, step):
        put(
            start,
            jnp.dot(
                normed, query_ref[:, start : start + step], preferred_element_type=jnp.float32
            ),
        )
    put(columns, jnp.dot(normed, keyval_ref[...], preferred_element_type=jnp.float32))
    put(columns + keyval_ref.shape[1], jnp.broadcast_to(square_sum, (rows, SQUARES)))


def project(near, far, gain, query_weight, keyval_weight):
    rows = near.shape[1]
    columns = query_weight.shape[1] + keyval_weight.shape[1] + SQUARES
    half = jax.ShapeDtypeStruct((rows // 2, columns), jnp.float32)
    return call(
        project_kernel,
        [half, half],
        [VMEM] * 5,
        [VMEM] * 2,
        [pltpu.VMEM((2 * near.shape[0],) + near.shape[1:], near.dtype)],
    )(near, far, gain[None], query_weight, keyval_weight)


def attend_kernel(
    features, lengths_ref, kept_ref, got_ref, cos_ref, sin_ref, key_ref, value_ref, out_ref,
    proj_scr, query_scr, score_scr, rows_scr,
):
    rows, positions, head_dim = key_ref.shape
    heads = query_scr.shape[1]
    query_cols = heads * head_dim
    scale = head_dim ** (-0.5)
    proj_scr[...] = kept_ref[...] + got_ref[...]

    def rotate(vectors, b):
        return vectors * cos_ref[b : b + 1] + pltpu.roll(vectors, head_dim // 2, 1) * sin_ref[
            b : b + 1
        ]

    queries, tops, news = [], [], []
    for b in range(rows):
        squares = proj_scr[b : b + 1, -SQUARES:]
        inv_scale = lax.rsqrt(squares / features + 1e-05)
        for h in range(heads):
            query_scr[b, h : h + 1, :] = (
                proj_scr[b : b + 1, h * head_dim : (h + 1) * head_dim] * inv_scale
            )
        query = rotate(query_scr[b], b).astype(jnp.bfloat16)
        new_key = proj_scr[b : b + 1, query_cols : query_cols + head_dim] * inv_scale
        new_key = rotate(jnp.broadcast_to(new_key, (8, head_dim)), b)[:1].astype(jnp.bfloat16)
        new_value = proj_scr[b : b + 1, query_cols + head_dim : query_cols + 2 * head_dim]
        new_value = (new_value * inv_scale).astype(jnp.bfloat16).astype(jnp.float32)
        self_score = (
            jnp.sum(
                query.astype(jnp.float32) * new_key.astype(jnp.float32), axis=1, keepdims=True
            )
            * scale
        )
        queries.append(query)
        news.append((self_score, new_value))
        tops.append(jnp.full((heads, CHUNK), masked_score, jnp.float32))
    for start in range(0, positions, CHUNK):
        for b in range(rows):
            scores = (
                lax.dot_general(
                    queries[b],
                    key_ref[b, start : start + CHUNK, :],
                    (((1,), (1,)), ((), ())),
                    preferred_element_type=jnp.float32,
                )
                * scale
            )
            place = start + lax.broadcasted_iota(jnp.int32, scores.shape, 1)
            scores = jnp.where(place < lengths_ref[b : b + 1, :1], scores, masked_score)
            score_scr[b, :, start : start + CHUNK] = scores
            tops[b] = jnp.maximum(tops[b], scores)
    sums, numers = [], []
    for b, (self_score, new_value) in enumerate(news):
        tops[b] = jnp.maximum(jnp.max(tops[b], axis=1, keepdims=True), self_score)
        sums.append(jnp.zeros((heads, CHUNK), jnp.float32))
        numers.append(jnp.exp(self_score - tops[b]) * new_value)
    for start in range(0, positions, CHUNK):
        for b in range(rows):
            expos = jnp.exp(score_scr[b, :, start : start + CHUNK] - tops[b])
            sums[b] = sums[b] + expos
            numers[b] = numers[b] + jnp.dot(
                expos.astype(jnp.bfloat16),
                value_ref[b, start : start + CHUNK, :],
                preferred_element_type=jnp.float32,
            )
    for b, (self_score, new_value) in enumerate(news):
        totals = jnp.sum(sums[b], axis=1, keepdims=True) + jnp.exp(self_score - tops[b])
        attended = numers[b] / totals
        for h in range(heads):
            rows_scr[b : b + 1, h * head_dim : (h + 1) * head_dim] = attended[h : h + 1, :]
    out_ref[...] = rows_scr[...].astype(jnp.bfloat16)


def attend(lengths, kept, got, cosine, sine, key_cache, value_cache, features, heads):
    rows, positions, head_dim = key_cache.shape
    return call(
        functools.partial(attend_kernel, features),
        jax.ShapeDtypeStruct((rows, heads * head_dim), jnp.bfloat16),
        [VMEM] * 7,
        VMEM,
        [
            pltpu.VMEM(kept.shape, jnp.float32),
            pltpu.VMEM((rows, heads, head_dim), jnp.float32),
            pltpu.VMEM((rows, heads, positions), jnp.float32),
            pltpu.VMEM((rows, heads * head_dim), jnp.float32),
        ],
        cost=2.2,
    )(lengths, kept, got, cosine, sine, key_cache, value_cache)


def mix_kernel(own_ref, other_ref, weight_ref, kept_ref, sent_ref, blocks_scr):
    rows = 2 * own_ref.shape[0]
    shape = (rows, rows)
    order = batch_row(lax.broadcasted_iota(jnp.int32, shape, 1))
    order = jnp.where(order == lax.broadcasted_iota(jnp.int32, shape, 0), 1.0, 0.0)
    attended = jnp.dot(
        order.astype(jnp.bfloat16),
        jnp.concatenate([own_ref[...], other_ref[...]], axis=0),
        preferred_element_type=jnp.float32,
    ).astype(jnp.bfloat16)
    step, width = 256, kept_ref.shape[2]
    for start in range(0, weight_ref.shape[1], step):
        mixed = jnp.dot(
            attended, weight_ref[:, start : start + step], preferred_element_type=jnp.float32
        )
        for k in range(step // width):
            blocks_scr[start // width + k] = mixed[:, k * width : (k + 1) * width]
    x_low, z = lax.axis_index("col") >> 2, lax.axis_index("col") & 3
    half = kept_ref.shape[0]
    for place in range(half):
        kept_ref[place] = blocks_scr[((x_low ^ (place & 1)) << 2) | (z ^ (place >> 1))]
        away = place + half
        sent_ref[place] = blocks_scr[((x_low ^ (away & 1)) << 2) | (z ^ (away >> 1))]


def mix(own, other, out_weight):
    rows, width = 2 * own.shape[0], out_weight.shape[1] // 8
    half = jax.ShapeDtypeStruct((4, rows, width), jnp.float32)
    return call(
        mix_kernel,
        [half, half],
        [VMEM] * 3,
        [VMEM] * 2,
        [pltpu.VMEM((8, rows, width), jnp.float32)],
        cost=2.2,
    )(own, other, out_weight)


SAME, OTHER = "same", "other"


def pick(piece_ref, slot, base=0):
    if slot == SAME:
        slot = lax.axis_index("row") & 1
    elif slot == OTHER:
        slot = (lax.axis_index("row") & 1) ^ 1
    return piece_ref.at[base + slot]


def start_and_wait(copies):
    for copy in copies:
        copy.start()
    for copy in copies:
        copy.wait()


def chip_pair(chunks, dy, dx):
    row = lax.axis_index("row")
    chip = ((((row >> 2) + dy) & 3) << 1) | (((row >> 1) & 1) ^ dx)
    return lax.dynamic_slice_in_dim(chunks, chip * 2, 2, 0)


def stage_kernel(groups, chunks_ref, *refs):
    pieces, (buffer, in_sems, out_sems) = refs[: len(groups)], refs[len(groups) :]
    row = lax.axis_index("row")
    copies = []
    for piece, group in zip(pieces, groups):
        for i, (dy, dx, core) in enumerate(group):
            chip = ((((row >> 2) + dy) & 3) << 1) | (((row >> 1) & 1) ^ dx)
            k = len(copies)
            copies.append(
                (
                    pltpu.make_async_copy(
                        chunks_ref.at[(chip << 1) | core], buffer.at[k], in_sems.at[k]
                    ),
                    pltpu.make_async_copy(buffer.at[k], piece.at[i], out_sems.at[k]),
                )
            )
    for fetch, _ in copies:
        fetch.start()
    for fetch, store in copies:
        fetch.wait()
        store.start()
    for _, store in copies:
        store.wait()


def stage(chunks, groups):
    count = sum(len(group) for group in groups)
    return call(
        functools.partial(stage_kernel, groups),
        [like(chunks, len(group)) for group in groups],
        [HBM],
        [HBM] * len(groups),
        [
            pltpu.VMEM((count,) + chunks.shape[1:], chunks.dtype),
            pltpu.SemaphoreType.DMA((count,)),
            pltpu.SemaphoreType.DMA((count,)),
        ],
        60,
    )(chunks)


def pack_kernel(count, slots, *refs):
    pieces, out_ref, sems = refs[:count], refs[-2], refs[-1]
    start_and_wait(
        [
            pltpu.make_async_copy(pick(pieces[p], *at), out_ref.at[k], sems.at[k])
            for k, (p, *at) in enumerate(slots)
        ]
    )


def pack(pieces, slots):
    return call(
        functools.partial(pack_kernel, len(pieces), slots),
        like(pieces[0], len(slots)),
        [ANYWHERE] * len(pieces),
        ANYWHERE,
        [pltpu.SemaphoreType.DMA((len(slots),))],
        1,
    )(*pieces)


def place_kernel(count, slots, *refs):
    pieces, relaid_ref, sems = refs[:count], refs[-2], refs[-1]
    row = lax.axis_index("row")
    copies = []
    for k, (piece, slot, dy, dx, other) in enumerate(slots):
        chip = ((((row >> 2) - dy) & 3) << 1) | (((row >> 1) & 1) ^ dx)
        column = pl.multiple_of(((chip << 1) | ((row & 1) ^ other)) * HD, HD)
        copies.append(
            pltpu.make_async_copy(
                pick(pieces[piece], slot), relaid_ref.at[:, pl.ds(column, HD)], sems.at[k]
            )
        )
    start_and_wait(copies)


def place(pieces, slots, relaid):
    rows, width = pieces[0].shape[1:]
    first = relaid is None
    return call(
        functools.partial(place_kernel, len(pieces), slots),
        jax.ShapeDtypeStruct((rows, 16 * width), jnp.bfloat16),
        [VMEM] * len(pieces) + ([] if first else [HBM]),
        HBM,
        [pltpu.SemaphoreType.DMA((len(slots),))],
        6,
        input_output_aliases={} if first else {len(pieces): 0},
    )(*pieces, *([] if first else [relaid]))


def body(
    tokens,
    norm_gain,
    query_weight,
    keyval_weight,
    out_weight,
    key_cache,
    value_cache,
    lengths,
    next_query,
):
    heads = query_weight.shape[1] // HD
    features = query_weight.shape[0] * lax.axis_size("row")
    cosine, sine = rotary_factors(lengths, HD)
    lengths = jnp.broadcast_to(lengths[:, None], cosine.shape)
    chunks = next_query.reshape(16, -1, next_query.shape[1])

    def pair(dy, dx):
        return [(dy, dx, 0), (dy, dx, 1)]

    to_a, to_b, to_c, to_e = stage(
        chunks,
        [
            [(dy, dx, core) for core in range(2)]
            for dy, dx in ((1, 0), (3, 0), (2, 0), (1, 1))
        ],
    )
    got_a, got_b, got_c = shift_y(to_a, 1), shift_y(to_b, 3), shift_y(to_c, 2)

    other = flip(tokens[None], "col", X_LOW)
    feats = fetch(tokens[None])
    other, feats, to_e, cosine, sine, lengths = tie(other, feats, to_e, cosine, sine, lengths)
    via_e = flip(to_e, "row", X_HALF)
    feats = join(feats, other, 3)
    other = flip(feats, "col", Z_NEAR)
    other, chunks = tie(other, chunks)
    own, to_d, to_f = [chip_pair(chunks, *at) for at in ((0, 0), (0, 1), (3, 1))]
    feats = join(feats, other, 1.2)
    other = flip(feats, "col", Z_FAR)
    other, chunks = tie(other, chunks)
    to_g = chip_pair(chunks, 2, 1)
    kept, sent = project(feats, other, norm_gain, query_weight, keyval_weight)
    got = flip(sent, "row", CORE)
    got, via_e, own, to_d, to_f, to_g = tie(got, via_e, own, to_d, to_f, to_g)
    kept, sent = add_halves(kept, got)
    got = flip(sent, "row", X_HALF)
    via_f = flip(to_f, "row", X_HALF)
    got, got_a, got_b, got_c = tie(got, got_a, got_b, got_c)
    swapped = pack(
        [own, got_a, got_b, got_c, to_d, via_e, to_g], [(k, OTHER) for k in range(7)]
    )
    swapped = flip(swapped, "row", CORE)
    kept, sent = add_halves(kept, got, 26)
    got = flip(sent, "row", Y_FAR)
    kept, sent = add_halves(kept, got)
    got = flip(sent, "row", Y_NEAR)
    via_g = flip(pack([to_g, swapped], [(0, SAME), (1, 6)]), "row", X_HALF)
    attended = attend(
        lengths, kept, got, cosine, sine, key_cache, value_cache, features, heads
    )
    other = flip(attended, "row", Y_NEAR)
    other, via_f = tie(other, via_f)
    via_e = pack([via_e, swapped], [(0, SAME), (1, 5)])
    attended = join(attended, other, 3)
    other = flip(attended, "row", Y_FAR)
    got_e, got_f = shift_y(via_e, 1), shift_y(via_f, 3)
    via_g, other = tie(via_g, other)
    attended = join(attended, other, 4.5)
    other = flip(attended, "row", X_HALF)
    got_d = flip(pack([to_d, swapped], [(0, SAME), (1, 4)]), "row", X_HALF)
    attended = join(attended, other, 1.2)
    other = flip(attended, "row", CORE)
    relaid = place(
        [own, got_a, got_b, got_c, swapped],
        [(k, SAME, dy, 0, 0) for k, dy in enumerate((0, 1, 3, 2))]
        + [(4, k, dy, 0, 1) for k, dy in enumerate((0, 1, 3, 2))],
        None,
    )
    kept, sent = mix(attended, other, out_weight)
    got = flip(sent, "col", Z_FAR)
    got_g = shift_y(via_g, 2)
    got, got_e, got_f = tie(got, got_e, got_f)
    swap_last = flip(pack([got_f], [(0, OTHER)]), "row", CORE)
    kept, sent = add_halves(kept, got, 0.3)
    got = flip(sent, "col", Z_NEAR)
    got, got_d, relaid = tie(got, got_d, relaid)
    kept, sent = add_halves(kept, got)
    got = flip(sent, "col", X_LOW)
    relaid = place(
        [got_d, got_e, got_f],
        [(0, 0, 0, 1, 0), (1, 0, 1, 1, 0), (2, SAME, 3, 1, 0), (0, 1, 0, 1, 1), (1, 1, 1, 1, 1)],
        relaid,
    )
    got, relaid = tie(got, relaid)
    mixed = (kept + got)[0].astype(jnp.bfloat16)
    relaid = place(
        [got_g, swap_last],
        [(0, 0, 2, 1, 0), (0, 1, 2, 1, 1), (1, 0, 3, 1, 1)],
        relaid,
    )
    return (mixed, relaid)


def solution(mesh):
    in_specs = (
        P(None, ("row", "col")),
        P("row"),
        P("row", "col"),
        P("row", "col"),
        P("col", "row"),
        P("row", None, "col"),
        P("row", None, "col"),
        P("row"),
        P(None, ("col", "row")),
    )
    out_specs = (P(None, ("row", "col")), P("row", "col"))
    return jax.shard_map(body, mesh=mesh, in_specs=in_specs, out_specs=out_specs, check_vma=False)
```
